32 devices in a mesh: expert: 8 (over y, x, core), etp: 4 (over z).
Axes of the slice: x: 2, y: 2, z: 4, core: 2. Of those that a mesh axis runs over, the one named last changes fastest.
Arguments:
- tokens: bfloat16 [1024, 2048], P('expert'), may hold values from -6 to 6
- out_grad: bfloat16 [1024, 2048], P('expert'), may hold values from -6 to 6
- routes: int32 [1024, 2], P('expert'), may hold values from 0 to 7, as said below
- combine_weights: float32 [1024, 2], P('expert'), may hold values from 0.2 to 1
- w_gate: bfloat16 [8, 2048, 3584], P('expert', None, 'etp'), may hold values from -0.125 to 0.125
- w_up: bfloat16 [8, 2048, 3584], P('expert', None, 'etp'), may hold values from -0.125 to 0.125
- w_down: bfloat16 [8, 3584, 2048], P('expert', 'etp'), may hold values from -0.09375 to 0.09375
Outputs:
- mixed: bfloat16 [1024, 2048], P('expert')
- tokens_grad: bfloat16 [1024, 2048], P('expert')
- combine_grad: float32 [1024, 2], P('expert')
- gate_weight_grad: bfloat16 [8, 2048, 3584], P('expert', None, 'etp')
- up_weight_grad: bfloat16 [8, 2048, 3584], P('expert', None, 'etp')
- down_weight_grad: bfloat16 [8, 3584, 2048], P('expert', 'etp')
The draws below stay inside these ranges and needn't reach their ends.
Inputs may be any that keep to these rules, and one draw needn't show every extreme that they name: `routes`: each token names two different experts. No expert is named by more than 32 tokens of one group of 128 consecutive tokens, and one expert, the same in every group, is named by exactly 32 tokens of each group.
All inputs are finite; a program needn't handle non-finite values.
Results may differ from the reference program's by a relative error of at most 0.02.
Values may be sent and summed in bfloat16 or wider, within the bound.
A program may use at most 128 MiB of HBM per device.

```python
import jax
import jax.numpy as jnp
from jax import lax

D = 2048
FF_DEV = 896
TOP = 2
TOK_GRP = 128
EXPERTS = 8
BLOCKS = 4
FF = 3584
CAP = 32
TOKENS = 1024


def route_block(block_key, hot_expert):
    count_key, order_key, swap_key, token_key = jax.random.split(block_key, 4)
    weights = jax.random.randint(count_key, (EXPERTS - 1,), 2, 5)
    remaining = 2 * TOK_GRP - CAP
    base = jnp.minimum(remaining * weights // jnp.sum(weights), CAP)
    leftover = remaining - jnp.sum(base)
    room = CAP - base
    before = jnp.cumsum(room) - room
    extra = jnp.clip(leftover - before, 0, room)
    other_counts = base + extra
    order = jax.random.permutation(order_key, EXPERTS - 1)
    other_ids = (hot_expert + 1 + order) % EXPERTS
    run_ids = jnp.concatenate([jnp.reshape(hot_expert, (1,)), other_ids]).astype(jnp.int32)
    run_counts = jnp.concatenate([jnp.full((1,), CAP, jnp.int32), other_counts.astype(jnp.int32)])
    run_ends = jnp.cumsum(run_counts)
    positions = jnp.arange(2 * TOK_GRP, dtype=jnp.int32)
    run_index = jnp.sum((positions[:, None] >= run_ends[None, :]).astype(jnp.int32), axis=1)
    slot_ids = run_ids[run_index]
    paired = jnp.stack([slot_ids[:TOK_GRP], slot_ids[TOK_GRP:]], axis=1)
    swapped = jax.random.randint(swap_key, (TOK_GRP,), 0, 2)
    paired = jnp.where(swapped[:, None] == 1, paired[:, ::-1], paired)
    shuffle = jax.random.permutation(token_key, TOK_GRP)
    return paired[shuffle]


def draw_routes(key, part):
    group_count = TOKENS // TOK_GRP
    hot_key, rest_key = jax.random.split(jax.random.fold_in(key, 11))
    hot_expert = jax.random.randint(hot_key, (), 0, EXPERTS)
    block_keys = jax.random.split(rest_key, group_count)
    blocks = jax.vmap(lambda block_key: route_block(block_key, hot_expert))(block_keys)
    return blocks.reshape(TOKENS, TOP).astype(jnp.int32)


def block_scale(stream_key, dims, cuts, least, high):
    def one(dim, parts):
        heights = jax.random.uniform(jax.random.fold_in(jax.random.fold_in(stream_key, 6), dim), (parts,), jnp.float32, least / len(cuts), high / len(cuts))
        return jnp.repeat(jnp.exp(heights), dims[dim] // parts).reshape((-1,) + (1,) * (len(dims) - dim - 1))

    level = one(*cuts[0])
    for cut in cuts[1:]:
        level = level * one(*cut)
    return level


def noise(own_key, shape, width, bound, shards=(), held_as=jnp.bfloat16):
    loudness = block_scale(own_key, shape, shards, -0.22, 0.18) if shards else 1.0
    entries = jax.random.normal(own_key, shape, jnp.float32) * width * loudness
    return jnp.minimum(jnp.maximum(entries, -bound), bound).astype(held_as)


def setup_inputs(seed: int = 0) -> dict:
    keys = jax.random.split(jax.random.key(seed), 8)
    tokens = noise(keys[0], (TOKENS, D), 1.0, 6.0, ((0, 8),))
    out_grad = noise(keys[1], (TOKENS, D), 1.0, 6.0, ((0, 8),))
    routes = draw_routes(jax.random.fold_in(keys[7], 71), 0)
    combine_weights = jnp.clip(0.2 + 0.8 * jax.random.uniform(keys[3], (TOKENS, TOP), jnp.float32) ** block_scale(keys[3], (TOKENS, TOP), ((0, 8),), -0.2, 0.2), 0.2, 1.0)
    w_gate = noise(keys[4], (EXPERTS, D, FF), D ** -0.5, 0.125, ((0, 8), (2, 4)))
    w_up = noise(keys[5], (EXPERTS, D, FF), D ** -0.5, 0.125, ((0, 8), (2, 4)))
    w_down = noise(keys[6], (EXPERTS, FF, D), FF ** -0.5, 0.09375, ((0, 8), (1, 4)))
    return {"tokens": tokens, "out_grad": out_grad, "routes": routes, "combine_weights": combine_weights, "w_gate": w_gate, "w_up": w_up, "w_down": w_down}


def slot_numbers(routes):
    grouped = routes.reshape(TOKENS // TOK_GRP, TOK_GRP * TOP)
    one_hot = (grouped[:, :, None] == jnp.arange(EXPERTS, dtype=jnp.int32)[None, None, :]).astype(jnp.int32)
    before = jnp.cumsum(one_hot, axis=1) - one_hot
    return jnp.sum(before * one_hot, axis=2).reshape(TOKENS, TOP)


def expert_pass(operands):
    rows_in, rows_grad, gate_w, up_w, down_w = operands
    row_count = rows_in.shape[0]
    gate_pre = jnp.dot(rows_in, gate_w, preferred_element_type=jnp.float32)
    up_pre = jnp.dot(rows_in, up_w, preferred_element_type=jnp.float32)
    gate_sig = jax.nn.sigmoid(gate_pre)
    swish = gate_pre * gate_sig
    hidden = (swish * up_pre).astype(jnp.bfloat16)

    def add_out(block, total):
        start = block * FF_DEV
        hidden_block = lax.dynamic_slice_in_dim(hidden, start, FF_DEV, 1)
        down_block = lax.dynamic_slice_in_dim(down_w, start, FF_DEV, 0)
        term = jnp.dot(hidden_block, down_block, preferred_element_type=jnp.float32)
        return total + lax.optimization_barrier(term.astype(jnp.bfloat16)).astype(jnp.float32)

    out_total = lax.fori_loop(0, BLOCKS, add_out, jnp.zeros((row_count, D), jnp.float32))
    hidden_grad = jnp.dot(rows_grad, down_w.T, preferred_element_type=jnp.float32)
    down_grad = jnp.dot(hidden.T, rows_grad, preferred_element_type=jnp.float32).astype(jnp.bfloat16)
    gate_grad = (hidden_grad * up_pre * gate_sig * (1.0 + gate_pre * (1.0 - gate_sig))).astype(jnp.bfloat16)
    up_grad = (hidden_grad * swish).astype(jnp.bfloat16)
    gate_weight_grad = jnp.dot(rows_in.T, gate_grad, preferred_element_type=jnp.float32).astype(jnp.bfloat16)
    up_weight_grad = jnp.dot(rows_in.T, up_grad, preferred_element_type=jnp.float32).astype(jnp.bfloat16)

    def add_input(block, total):
        start = block * FF_DEV
        gate_block = lax.dynamic_slice_in_dim(gate_grad, start, FF_DEV, 1)
        up_block = lax.dynamic_slice_in_dim(up_grad, start, FF_DEV, 1)
        gate_cols = lax.dynamic_slice_in_dim(gate_w, start, FF_DEV, 1)
        up_cols = lax.dynamic_slice_in_dim(up_w, start, FF_DEV, 1)
        term = jnp.dot(gate_block, gate_cols.T, preferred_element_type=jnp.float32)
        term = term + jnp.dot(up_block, up_cols.T, preferred_element_type=jnp.float32)
        return total + lax.optimization_barrier(term.astype(jnp.bfloat16)).astype(jnp.float32)

    input_total = lax.fori_loop(0, BLOCKS, add_input, jnp.zeros((row_count, D), jnp.float32))
    return (out_total.astype(jnp.bfloat16), input_total.astype(jnp.bfloat16),
            gate_weight_grad, up_weight_grad, down_grad)


def reference(tokens, out_grad, routes, combine_weights, w_gate, w_up, w_down):
    slots = slot_numbers(routes)
    group_of = (jnp.arange(TOKENS, dtype=jnp.int32) // TOK_GRP)[:, None]
    expert_rows = EXPERTS * CAP
    position = (routes * expert_rows + group_of * CAP + slots).astype(jnp.int32)
    pair_count = TOKENS * TOP
    source_index = jnp.full((EXPERTS * expert_rows,), pair_count, jnp.int32)
    source_index = source_index.at[position.reshape(-1)].set(jnp.arange(pair_count, dtype=jnp.int32))
    zero_row = jnp.zeros((1, D), jnp.bfloat16)
    padded_tokens = jnp.concatenate([tokens, zero_row], axis=0)
    scaled_grad = (combine_weights[:, :, None] * out_grad.astype(jnp.float32)[:, None, :]).astype(jnp.bfloat16)
    padded_grad = jnp.concatenate([scaled_grad.reshape(pair_count, D), zero_row], axis=0)
    rows_in = padded_tokens[source_index // TOP].reshape(EXPERTS, expert_rows, D)
    rows_grad = padded_grad[source_index].reshape(EXPERTS, expert_rows, D)
    out_rows, input_rows, gate_weight_grad, up_weight_grad, down_weight_grad = lax.map(
        expert_pass, (rows_in, rows_grad, w_gate, w_up, w_down))
    out_pairs = out_rows.reshape(EXPERTS * expert_rows, D)[position].astype(jnp.float32)
    input_pairs = input_rows.reshape(EXPERTS * expert_rows, D)[position].astype(jnp.float32)
    mixed = jnp.sum(combine_weights[:, :, None] * out_pairs, axis=1).astype(jnp.bfloat16)
    combine_grad = jnp.sum(out_grad.astype(jnp.float32)[:, None, :] * out_pairs, axis=2)
    tokens_grad = jnp.sum(input_pairs, axis=1).astype(jnp.bfloat16)
    return (mixed, tokens_grad, combine_grad, gate_weight_grad, up_weight_grad, down_weight_grad)
```

```python
import functools

import jax
import jax.numpy as jnp
from jax import lax
from jax.experimental import pallas as pl
from jax.experimental.pallas import tpu as pltpu
from jax.sharding import PartitionSpec as P

MESH = pl.DeviceIdType.MESH
BF16 = jnp.bfloat16
F32 = jnp.float32
CHUNK = 512
LANES = 128


def dot(left, right):
    return jnp.dot(left, right, preferred_element_type=F32)


def contract_last(left, right):
    return lax.dot_general(left, right, (((1,), (1,)), ((), ())), preferred_element_type=F32)


def contract_first(left, right):
    return lax.dot_general(left, right, (((0,), (0,)), ((), ())), preferred_element_type=F32)


def one_hot_places(routes_row, routes_col, cap, places):
    tokens = routes_row.shape[1]
    before_by = lax.broadcasted_iota(jnp.int32, (tokens, tokens), 0)
    before_at = lax.broadcasted_iota(jnp.int32, (tokens, tokens), 1)
    upper = (before_by < before_at).astype(F32).astype(BF16)
    lower = (before_by > before_at).astype(F32).astype(BF16)
    expert_down = lax.broadcasted_iota(jnp.int32, (LANES, tokens), 0)
    expert_across = lax.broadcasted_iota(jnp.int32, (tokens, LANES), 1)
    named_down = [(expert_down == routes_row[k : k + 1, :]).astype(F32) for k in range(2)]
    named_across = [(expert_across == routes_col[:, k : k + 1]).astype(F32) for k in range(2)]
    earlier_down = dot((named_down[0] + named_down[1]).astype(BF16), upper)
    earlier_across = dot(lower, (named_across[0] + named_across[1]).astype(BF16))
    start_down = earlier_down + expert_down.astype(F32) * cap
    start_across = earlier_across + expert_across.astype(F32) * cap
    place_down = lax.broadcasted_iota(jnp.int32, (places, tokens), 0).astype(F32)
    place_across = lax.broadcasted_iota(jnp.int32, (tokens, places), 1).astype(F32)
    scatter, gather = [], []
    for k in range(2):
        row = jnp.sum(named_down[k] * start_down, axis=0, keepdims=True)
        col = jnp.sum(named_across[k] * start_across, axis=1, keepdims=True)
        scatter.append((place_down == row).astype(F32).astype(BF16))
        gather.append((place_across == col).astype(F32).astype(BF16))
    return scatter, gather


def layer_kernel(
    experts,
    lines,
    tokens_ref,
    grad_ref,
    routes_row_ref,
    routes_col_ref,
    weights_ref,
    gate_hbm,
    up_hbm,
    down_hbm,
    mixed_ref,
    tokens_grad_ref,
    combine_ref,
    rows_out,
    rows_grad_out,
    hidden_out,
    gate_grad_out,
    up_grad_out,
    gate_w,
    up_w,
    down_w,
    send,
    rows,
    gate_pre,
    up_pre,
    hidden,
    gate_grad,
    up_grad,
    gather_mat,
    part,
    back,
    line_own,
    line_in,
    line_total,
    dot_own,
    dot_in,
    dot_total,
    load_sem,
    store_sem,
    send_sem,
    recv_sem,
    part_sem,
    back_sem,
    inner_sem,
    line_sem,
    outer_sem,
):
    token_count, features = tokens_ref.shape
    cap = token_count // 4
    places = experts * cap
    chunks = features // CHUNK
    me = lax.axis_index("expert")
    z = lax.axis_index("etp")
    half = lines // 2
    side = 1 - z // half
    inner = z + 2 * side - 1
    outer = z - 2 * side + 1
    has_outer = jnp.logical_and(z > 0, z < lines - 1)
    center = jnp.logical_or(z == half - 1, z == half)
    kind = jnp.where(center, 1, 0)

    loads = [
        pltpu.make_async_copy(src, dst, load_sem.at[i])
        for i, (src, dst) in enumerate(((gate_hbm, gate_w), (up_hbm, up_w), (down_hbm, down_w)))
    ]
    for load in loads:
        load.start()

    barrier = pltpu.get_barrier_semaphore()

    def greet(d, carry):
        peer = lax.rem(me + d, experts)
        pl.semaphore_signal(barrier, inc=1, device_id={"expert": peer}, device_id_type=MESH)
        return carry

    lax.fori_loop(1, experts, greet, 0)
    pl.semaphore_signal(barrier, inc=1, device_id={"etp": inner}, device_id_type=MESH)

    @pl.when(has_outer)
    def _():
        pl.semaphore_signal(barrier, inc=1, device_id={"etp": outer}, device_id_type=MESH)

    def block_of(index):
        return pl.ds(pl.multiple_of(index * cap, cap), cap)

    mine = block_of(me)

    def dispatch(i, peer, owner):
        return pltpu.make_async_remote_copy(
            src_ref=send.at[i, block_of(peer)],
            dst_ref=rows.at[i, block_of(owner)],
            send_sem=send_sem.at[i, peer],
            recv_sem=recv_sem.at[i, owner],
            device_id={"expert": peer},
            device_id_type=MESH,
        )

    def give_back(i, peer, owner):
        return pltpu.make_async_remote_copy(
            src_ref=part.at[i, block_of(peer)],
            dst_ref=back.at[i, block_of(owner)],
            send_sem=part_sem.at[i, peer],
            recv_sem=back_sem.at[i, owner],
            device_id={"expert": peer},
            device_id_type=MESH,
        )

    def each_peer(action):
        def body(d, carry):
            action(lax.rem(me + d, experts))
            return carry

        lax.fori_loop(1, experts, body, 0)

    scatter, gather = one_hot_places(routes_row_ref[...], routes_col_ref[...], cap, places)
    for k in range(2):
        gather_mat[k] = gather[k]
    scatter_both = scatter[0] + scatter[1]
    for c in range(chunks):
        cols = slice(c * CHUNK, (c + 1) * CHUNK)
        send[0, :, cols] = dot(scatter_both, tokens_ref[:, cols]).astype(BF16)

    pl.semaphore_wait(barrier, experts + jnp.where(has_outer, 1, 0))
    each_peer(lambda q: dispatch(0, q, me).start())
    rows[0, mine] = send[0, mine]
    for c in range(chunks):
        cols = slice(c * CHUNK, (c + 1) * CHUNK)
        value = grad_ref[:, cols].astype(F32)
        scaled = [(weights_ref[:, k : k + 1] * value).astype(BF16) for k in range(2)]
        send[1, :, cols] = (dot(scatter[0], scaled[0]) + dot(scatter[1], scaled[1])).astype(BF16)
    each_peer(lambda q: dispatch(1, q, me).start())
    rows[1, mine] = send[1, mine]

    loads[0].wait()
    loads[1].wait()
    loads[2].wait()
    each_peer(lambda q: dispatch(0, me, q).wait_recv())
    gate_pre[...] = dot(rows[0], gate_w[...])
    up_pre[...] = dot(rows[0], up_w[...])
    gate_value = gate_pre[...]
    hidden[...] = (gate_value * jax.nn.sigmoid(gate_value) * up_pre[...]).astype(BF16)
    for c in range(chunks):
        part[c] = dot(hidden[...], down_w[:, c * CHUNK : (c + 1) * CHUNK]).astype(BF16)
        each_peer(lambda q, c=c: give_back(c, q, me).start())
        back[c, mine] = part[c, mine]

    each_peer(lambda q: dispatch(1, me, q).wait_recv())
    hidden_grad = contract_last(rows[1], down_w[...])
    gate_value = gate_pre[...]
    sig = jax.nn.sigmoid(gate_value)
    gate_grad[...] = (
        hidden_grad * up_pre[...] * sig * (1.0 + gate_value * (1.0 - sig))
    ).astype(BF16)
    up_grad[...] = (hidden_grad * (gate_value * sig)).astype(BF16)
    for c in range(chunks):
        i = chunks + c
        rows_of = slice(c * CHUNK, (c + 1) * CHUNK)
        part[i] = (
            contract_last(gate_grad[...], gate_w[rows_of, :])
            + contract_last(up_grad[...], up_w[rows_of, :])
        ).astype(BF16)
        each_peer(lambda q, i=i: give_back(i, q, me).start())
        back[i, mine] = part[i, mine]

    stores = [
        pltpu.make_async_copy(src, dst, store_sem.at[i])
        for i, (src, dst) in enumerate(
            (
                (rows.at[0], rows_out),
                (rows.at[1], rows_grad_out),
                (hidden, hidden_out),
                (gate_grad, gate_grad_out),
                (up_grad, up_grad_out),
            )
        )
    ]
    for store in stores:
        store.start()

    last = 2 * chunks

    def line_refs(i):
        if i == last:
            return dot_own, dot_in.at[0], dot_in.at[1], dot_total
        return line_own.at[i], line_in.at[0, i], line_in.at[1, i], line_total.at[i]

    def to_inner(i):
        own = line_refs(i)[0]
        target = dot_in.at[kind] if i == last else line_in.at[kind, i]
        return pltpu.make_async_remote_copy(
            src_ref=own,
            dst_ref=target,
            send_sem=inner_sem.at[i],
            recv_sem=line_sem.at[kind, i],
            device_id={"etp": inner},
            device_id_type=MESH,
        )

    def to_outer(i):
        _, _, target, total = line_refs(i)
        return pltpu.make_async_remote_copy(
            src_ref=total,
            dst_ref=target,
            send_sem=outer_sem.at[i],
            recv_sem=line_sem.at[1, i],
            device_id={"etp": outer},
            device_id_type=MESH,
        )

    def arrived(i, which):
        own, _, _, _ = line_refs(i)
        target = line_refs(i)[1 + which]
        return pltpu.make_async_remote_copy(
            src_ref=own,
            dst_ref=target,
            send_sem=inner_sem.at[i],
            recv_sem=line_sem.at[which, i],
            device_id={"etp": inner},
            device_id_type=MESH,
        )

    def inward(i, value):
        own, from_outer, _, _ = line_refs(i)

        @pl.when(has_outer)
        def _():
            arrived(i, 0).wait_recv()
            own[...] = (value + from_outer[...].astype(F32)).astype(own.dtype)

        @pl.when(jnp.logical_not(has_outer))
        def _():
            own[...] = value.astype(own.dtype)

        to_inner(i).start()

    def outward(i):
        own, _, from_inner, total = line_refs(i)
        arrived(i, 1).wait_recv()

        @pl.when(center)
        def _():
            total[...] = (own[...].astype(F32) + from_inner[...].astype(F32)).astype(own.dtype)

        @pl.when(jnp.logical_not(center))
        def _():
            total[...] = from_inner[...]

        @pl.when(has_outer)
        def _():
            to_outer(i).start()

        if i < chunks:
            mixed_ref[:, i * CHUNK : (i + 1) * CHUNK] = total[...]
        elif i < last:
            c = i - chunks
            tokens_grad_ref[:, c * CHUNK : (c + 1) * CHUNK] = total[...]
        else:
            combine_ref[...] = total[...]

    order = list(range(chunks)) + [last] + list(range(chunks, last))
    weight = [weights_ref[:, k : k + 1] for k in range(2)]
    products = [None, None]
    waiting = []
    for i in order:
        if i == last:
            sums = [jnp.sum(product, axis=1, keepdims=True) for product in products]
            lane = lax.broadcasted_iota(jnp.int32, (token_count, LANES), 1)
            table = jnp.where(lane == 0, sums[0], jnp.where(lane == 1, sums[1], 0.0))
            inward(i, table.T[:8])
        else:
            each_peer(lambda q, i=i: give_back(i, me, q).wait_recv())
            if i < chunks:
                pairs = [dot(gather_mat[k], back[i]) for k in range(2)]
                value = grad_ref[:, i * CHUNK : (i + 1) * CHUNK].astype(F32)
                for k in range(2):
                    term = value * pairs[k]
                    for s in range(CHUNK // LANES):
                        piece = term[:, s * LANES : (s + 1) * LANES]
                        products[k] = piece if products[k] is None else products[k] + piece
                inward(i, weight[0] * pairs[0] + weight[1] * pairs[1])
            else:
                inward(i, dot(gather_mat[0] + gather_mat[1], back[i]))
        waiting.append(i)
        if len(waiting) > 2:
            outward(waiting.pop(0))
    for i in waiting:
        outward(i)

    for store in stores:
        store.wait()
    each_peer(lambda q: dispatch(0, q, me).wait_send())
    each_peer(lambda q: dispatch(1, q, me).wait_send())
    for i in range(last):
        each_peer(lambda q, i=i: give_back(i, q, me).wait_send())
    for i in range(last + 1):
        to_inner(i).wait_send()

    @pl.when(has_outer)
    def _():
        for i in range(last + 1):
            to_outer(i).wait_send()


def weight_grad_kernel(
    rows_ref, rows_grad_ref, hidden_ref, gate_ref, up_ref, gate_out, up_out, down_out, turned
):
    @pl.when(pl.program_id(0) == 0)
    def _():
        turned[...] = hidden_ref[...].T

    rows_t = rows_ref[...].T
    gate_out[...] = dot(rows_t, gate_ref[...]).astype(BF16)
    up_out[...] = dot(rows_t, up_ref[...]).astype(BF16)
    down_out[...] = dot(turned[...], rows_grad_ref[...]).astype(BF16)


def weight_grads(rows, rows_grad, hidden, gate_grad, up_grad):
    places, features = rows.shape
    units = hidden.shape[1]
    block = 256
    by_feature = pl.BlockSpec((places, block), lambda i: (0, i))
    whole = pl.BlockSpec((places, units), lambda i: (0, 0))
    tall = pl.BlockSpec((block, units), lambda i: (i, 0))
    wide = pl.BlockSpec((units, block), lambda i: (0, i))
    return pl.pallas_call(
        weight_grad_kernel,
        grid=(features // block,),
        in_specs=[by_feature, by_feature, whole, whole, whole],
        out_specs=[tall, tall, wide],
        out_shape=[
            jax.ShapeDtypeStruct((features, units), BF16),
            jax.ShapeDtypeStruct((features, units), BF16),
            jax.ShapeDtypeStruct((units, features), BF16),
        ],
        scratch_shapes=[pltpu.VMEM((units, places), BF16)],
        compiler_params=pltpu.CompilerParams(vmem_limit_bytes=32 << 20),
        cost_estimate=pl.CostEstimate(
            flops=6 * places * features * units,
            bytes_accessed=6 * features * units + 4 * places * features + 6 * places * units,
            transcendentals=0,
        ),
    )(rows, rows_grad, hidden, gate_grad, up_grad)


def shards(experts, lines, tokens, out_grad, routes, combine_weights, w_gate, w_up, w_down):
    token_count, features = tokens.shape
    units = w_gate.shape[2]
    cap = token_count // 4
    places = experts * cap
    chunks = features // CHUNK
    vmem = pl.BlockSpec(memory_space=pltpu.VMEM)
    hbm = pl.BlockSpec(memory_space=pl.ANY)
    dma = pltpu.SemaphoreType.DMA
    outs = pl.pallas_call(
        functools.partial(layer_kernel, experts, lines),
        in_specs=[vmem] * 5 + [hbm] * 3,
        out_specs=[vmem] * 3 + [hbm] * 5,
        out_shape=[
            jax.ShapeDtypeStruct((token_count, features), BF16),
            jax.ShapeDtypeStruct((token_count, features), BF16),
            jax.ShapeDtypeStruct((8, token_count), F32),
            jax.ShapeDtypeStruct((places, features), BF16),
            jax.ShapeDtypeStruct((places, features), BF16),
            jax.ShapeDtypeStruct((places, units), BF16),
            jax.ShapeDtypeStruct((places, units), BF16),
            jax.ShapeDtypeStruct((places, units), BF16),
        ],
        scratch_shapes=[
            pltpu.VMEM((features, units), BF16),
            pltpu.VMEM((features, units), BF16),
            pltpu.VMEM((units, features), BF16),
            pltpu.VMEM((2, places, features), BF16),
            pltpu.VMEM((2, places, features), BF16),
            pltpu.VMEM((places, units), F32),
            pltpu.VMEM((places, units), F32),
            pltpu.VMEM((places, units), BF16),
            pltpu.VMEM((places, units), BF16),
            pltpu.VMEM((places, units), BF16),
            pltpu.VMEM((2, token_count, places), BF16),
            pltpu.VMEM((2 * chunks, places, CHUNK), BF16),
            pltpu.VMEM((2 * chunks, places, CHUNK), BF16),
            pltpu.VMEM((2 * chunks, token_count, CHUNK), BF16),
            pltpu.VMEM((2, 2 * chunks, token_count, CHUNK), BF16),
            pltpu.VMEM((2 * chunks, token_count, CHUNK), BF16),
            pltpu.VMEM((8, token_count), F32),
            pltpu.VMEM((2, 8, token_count), F32),
            pltpu.VMEM((8, token_count), F32),
            dma((3,)),
            dma((5,)),
            dma((2, experts)),
            dma((2, experts)),
            dma((2 * chunks, experts)),
            dma((2 * chunks, experts)),
            dma((2 * chunks + 1,)),
            dma((2, 2 * chunks + 1)),
            dma((2 * chunks + 1,)),
        ],
        compiler_params=pltpu.CompilerParams(
            collective_id=0, has_side_effects=True, vmem_limit_bytes=56 << 20
        ),
        cost_estimate=pl.CostEstimate(
            flops=12 * places * features * units,
            bytes_accessed=6 * features * units,
            transcendentals=2 * places * units,
        ),
    )(tokens, out_grad, routes.T, routes, combine_weights, w_gate[0], w_up[0], w_down[0])
    mixed, tokens_grad, combine, rows, rows_grad, hidden, gate_grad, up_grad = outs
    gate_wg, up_wg, down_wg = weight_grads(rows, rows_grad, hidden, gate_grad, up_grad)
    return mixed, tokens_grad, combine[:2].T, gate_wg[None], up_wg[None], down_wg[None]


def solution(mesh):
    rows = P("expert", None)
    columns = P("expert", None, "etp")
    return jax.shard_map(
        functools.partial(shards, mesh.shape["expert"], mesh.shape["etp"]),
        mesh=mesh,
        in_specs=(rows, rows, rows, rows, columns, columns, P("expert", "etp", None)),
        out_specs=(rows, rows, rows, columns, columns, P("expert", "etp", None)),
        check_vma=False,
    )
```

```python
import functools

import jax
import jax.numpy as jnp
from jax import lax
from jax.experimental import pallas as pl
from jax.experimental.pallas import tpu as pltpu
from jax.sharding import PartitionSpec as P

MESH = pl.DeviceIdType.MESH
BF16 = jnp.bfloat16
F32 = jnp.float32
CHUNK = 256
LANES = 128
LAG = 2


def dot(left, right):
    return jnp.dot(left, right, preferred_element_type=F32)


def contract_last(left, right):
    return lax.dot_general(left, right, (((1,), (1,)), ((), ())), preferred_element_type=F32)


def contract_first(left, right):
    return lax.dot_general(left, right, (((0,), (0,)), ((), ())), preferred_element_type=F32)


def one_hot_places(routes_row, routes_col, cap, places):
    tokens = routes_row.shape[1]
    before_by = lax.broadcasted_iota(jnp.int32, (tokens, tokens), 0)
    before_at = lax.broadcasted_iota(jnp.int32, (tokens, tokens), 1)
    upper = (before_by < before_at).astype(F32).astype(BF16)
    lower = (before_by > before_at).astype(F32).astype(BF16)
    expert_down = lax.broadcasted_iota(jnp.int32, (LANES, tokens), 0)
    expert_across = lax.broadcasted_iota(jnp.int32, (tokens, LANES), 1)
    named_down = [(expert_down == routes_row[k : k + 1, :]).astype(F32) for k in range(2)]
    named_across = [
        (expert_across.astype(F32) == routes_col[:, k : k + 1]).astype(F32) for k in range(2)
    ]
    earlier_down = dot((named_down[0] + named_down[1]).astype(BF16), upper)
    earlier_across = dot(lower, (named_across[0] + named_across[1]).astype(BF16))
    start_down = earlier_down + expert_down.astype(F32) * cap
    start_across = earlier_across + expert_across.astype(F32) * cap
    place_down = lax.broadcasted_iota(jnp.int32, (places, tokens), 0).astype(F32)
    place_across = lax.broadcasted_iota(jnp.int32, (tokens, places), 1).astype(F32)
    scatter, gather = [], []
    for k in range(2):
        row = jnp.sum(named_down[k] * start_down, axis=0, keepdims=True)
        col = jnp.sum(named_across[k] * start_across, axis=1, keepdims=True)
        scatter.append((place_down == row).astype(F32).astype(BF16))
        gather.append((place_across == col).astype(F32).astype(BF16))
    return scatter, gather


def layer_kernel(
    experts,
    lines,
    tokens_ref,
    grad_ref,
    routes_ref,
    weights_ref,
    gate_hbm,
    up_hbm,
    down_hbm,
    mixed_ref,
    tokens_grad_ref,
    combine_ref,
    rows_t_out,
    rows_grad_out,
    hidden_t_out,
    gate_grad_out,
    up_grad_out,
    gate_w,
    up_w,
    down_w,
    send,
    rows,
    gate_pre,
    up_pre,
    hidden,
    gate_grad,
    up_grad,
    rows_t,
    hidden_t,
    gather_mat,
    part,
    back,
    line_own,
    line_in,
    line_total,
    dot_own,
    dot_in,
    dot_total,
    load_sem,
    store_sem,
    send_sem,
    recv_sem,
    part_sem,
    back_sem,
    inner_sem,
    line_sem,
    outer_sem,
):
    token_count, features = tokens_ref.shape
    cap = token_count // 4
    places = experts * cap
    chunks = features // CHUNK
    me = lax.axis_index("expert")
    z = lax.axis_index("etp")
    half = lines // 2
    side = 1 - z // half
    inner = z + 2 * side - 1
    outer = z - 2 * side + 1
    has_outer = jnp.logical_and(z > 0, z < lines - 1)
    center = jnp.logical_or(z == half - 1, z == half)
    kind = jnp.where(center, 1, 0)

    loads = [
        pltpu.make_async_copy(src, dst, load_sem.at[i])
        for i, (src, dst) in enumerate(((gate_hbm, gate_w), (up_hbm, up_w), (down_hbm, down_w)))
    ]
    for load in loads:
        load.start()

    barrier = pltpu.get_barrier_semaphore()

    def greet(d, carry):
        peer = lax.rem(me + d, experts)
        pl.semaphore_signal(barrier, inc=1, device_id={"expert": peer}, device_id_type=MESH)
        return carry

    lax.fori_loop(1, experts, greet, 0)
    pl.semaphore_signal(barrier, inc=1, device_id={"etp": inner}, device_id_type=MESH)

    @pl.when(has_outer)
    def _():
        pl.semaphore_signal(barrier, inc=1, device_id={"etp": outer}, device_id_type=MESH)

    def block_of(index):
        return pl.ds(pl.multiple_of(index * cap, cap), cap)

    mine = block_of(me)

    def dispatch(i, peer, owner):
        return pltpu.make_async_remote_copy(
            src_ref=send.at[i, block_of(peer)],
            dst_ref=rows.at[i, block_of(owner)],
            send_sem=send_sem.at[i, peer],
            recv_sem=recv_sem.at[i, owner],
            device_id={"expert": peer},
            device_id_type=MESH,
        )

    def give_back(i, peer, owner):
        return pltpu.make_async_remote_copy(
            src_ref=part.at[i, block_of(peer)],
            dst_ref=back.at[i, block_of(owner)],
            send_sem=part_sem.at[i, peer],
            recv_sem=back_sem.at[i, owner],
            device_id={"expert": peer},
            device_id_type=MESH,
        )

    def each_peer(action):
        def body(d, carry):
            action(lax.rem(me + d, experts))
            return carry

        lax.fori_loop(1, experts, body, 0)

    sub = lax.broadcasted_iota(jnp.int32, (LANES, token_count), 0)
    table = jnp.where(sub == 0, routes_ref[0:1, :], routes_ref[1:2, :]).astype(F32)
    table = jnp.where(sub == 2, weights_ref[0:1, :], table)
    table = jnp.where(sub == 3, weights_ref[1:2, :], table).T
    weight = [table[:, 2 + k : 3 + k] for k in range(2)]
    scatter, gather = one_hot_places(routes_ref[...], table, cap, places)
    for k in range(2):
        gather_mat[k] = gather[k]
    scatter_both = scatter[0] + scatter[1]
    for c in range(chunks):
        cols = slice(c * CHUNK, (c + 1) * CHUNK)
        send[0, :, cols] = dot(scatter_both, tokens_ref[:, cols]).astype(BF16)

    pl.semaphore_wait(barrier, experts + jnp.where(has_outer, 1, 0))
    each_peer(lambda q: dispatch(0, q, me).start())
    rows[0, mine] = send[0, mine]
    for c in range(chunks):
        cols = slice(c * CHUNK, (c + 1) * CHUNK)
        value = grad_ref[:, cols].astype(F32)
        scaled = [(weight[k] * value).astype(BF16) for k in range(2)]
        send[1, :, cols] = (dot(scatter[0], scaled[0]) + dot(scatter[1], scaled[1])).astype(BF16)
    each_peer(lambda q: dispatch(1, q, me).start())
    rows[1, mine] = send[1, mine]

    loads[0].wait()
    loads[1].wait()
    loads[2].wait()
    each_peer(lambda q: dispatch(0, me, q).wait_recv())
    gate_pre[...] = dot(rows[0], gate_w[...])
    up_pre[...] = dot(rows[0], up_w[...])
    gate_value = gate_pre[...]
    hidden[...] = (gate_value * jax.nn.sigmoid(gate_value) * up_pre[...]).astype(BF16)
    for c in range(chunks):
        part[c] = dot(hidden[...], down_w[:, c * CHUNK : (c + 1) * CHUNK]).astype(BF16)
        each_peer(lambda q, c=c: give_back(c, q, me).start())
        back[c, mine] = part[c, mine]

    hidden_t[...] = hidden[...].T
    for c in range(chunks):
        cols = slice(c * CHUNK, (c + 1) * CHUNK)
        rows_t[cols, :] = rows[0, :, cols].T

    each_peer(lambda q: dispatch(1, me, q).wait_recv())
    hidden_grad = contract_last(rows[1], down_w[...])
    gate_value = gate_pre[...]
    sig = jax.nn.sigmoid(gate_value)
    gate_grad[...] = (
        hidden_grad * up_pre[...] * sig * (1.0 + gate_value * (1.0 - sig))
    ).astype(BF16)
    up_grad[...] = (hidden_grad * (gate_value * sig)).astype(BF16)
    stores = [
        pltpu.make_async_copy(src, dst, store_sem.at[i])
        for i, (src, dst) in enumerate(
            (
                (rows_t, rows_t_out),
                (rows.at[1], rows_grad_out),
                (hidden_t, hidden_t_out),
                (gate_grad, gate_grad_out),
                (up_grad, up_grad_out),
            )
        )
    ]
    for store in stores:
        store.start()

    last = 2 * chunks

    def line_refs(i):
        if i == last:
            return dot_own, dot_in.at[0], dot_in.at[1], dot_total
        return line_own.at[i], line_in.at[0, i], line_in.at[1, i], line_total.at[i]

    def to_inner(i):
        own = line_refs(i)[0]
        target = dot_in.at[kind] if i == last else line_in.at[kind, i]
        return pltpu.make_async_remote_copy(
            src_ref=own,
            dst_ref=target,
            send_sem=inner_sem.at[i],
            recv_sem=line_sem.at[kind, i],
            device_id={"etp": inner},
            device_id_type=MESH,
        )

    def to_outer(i):
        _, _, target, total = line_refs(i)
        return pltpu.make_async_remote_copy(
            src_ref=total,
            dst_ref=target,
            send_sem=outer_sem.at[i],
            recv_sem=line_sem.at[1, i],
            device_id={"etp": outer},
            device_id_type=MESH,
        )

    def arrived(i, which):
        own, _, _, _ = line_refs(i)
        target = line_refs(i)[1 + which]
        return pltpu.make_async_remote_copy(
            src_ref=own,
            dst_ref=target,
            send_sem=inner_sem.at[i],
            recv_sem=line_sem.at[which, i],
            device_id={"etp": inner},
            device_id_type=MESH,
        )

    def inward(i, value):
        own, from_outer, _, _ = line_refs(i)

        @pl.when(has_outer)
        def _():
            arrived(i, 0).wait_recv()
            own[...] = (value + from_outer[...].astype(F32)).astype(own.dtype)

        @pl.when(jnp.logical_not(has_outer))
        def _():
            own[...] = value.astype(own.dtype)

        to_inner(i).start()

    def outward(i):
        own, _, from_inner, total = line_refs(i)
        arrived(i, 1).wait_recv()

        @pl.when(center)
        def _():
            total[...] = (own[...].astype(F32) + from_inner[...].astype(F32)).astype(own.dtype)

        @pl.when(jnp.logical_not(center))
        def _():
            total[...] = from_inner[...]

        @pl.when(has_outer)
        def _():
            to_outer(i).start()

        if i < chunks:
            mixed_ref[:, i * CHUNK : (i + 1) * CHUNK] = total[...]
        elif i < last:
            c = i - chunks
            tokens_grad_ref[:, c * CHUNK : (c + 1) * CHUNK] = total[...]
        else:
            combine_ref[...] = total[:2]

    products = [None, None]
    for i in range(chunks):
        j = chunks + i
        rows_of = slice(i * CHUNK, (i + 1) * CHUNK)
        part[j] = (
            contract_last(gate_grad[...], gate_w[rows_of, :])
            + contract_last(up_grad[...], up_w[rows_of, :])
        ).astype(BF16)
        each_peer(lambda q, j=j: give_back(j, q, me).start())
        back[j, mine] = part[j, mine]
        each_peer(lambda q, i=i: give_back(i, me, q).wait_recv())
        pairs = [dot(gather_mat[k], back[i]) for k in range(2)]
        value = grad_ref[:, rows_of].astype(F32)
        for k in range(2):
            term = value * pairs[k]
            for s in range(CHUNK // LANES):
                piece = term[:, s * LANES : (s + 1) * LANES]
                products[k] = piece if products[k] is None else products[k] + piece
        inward(i, weight[0] * pairs[0] + weight[1] * pairs[1])
        if i >= LAG:
            outward(i - LAG)
    sums = [jnp.sum(product, axis=1, keepdims=True) for product in products]
    lane = lax.broadcasted_iota(jnp.int32, (token_count, LANES), 1)
    inward(last, jnp.where(lane == 0, sums[0], jnp.where(lane == 1, sums[1], 0.0)).T[:8])
    waiting = list(range(chunks - LAG, chunks)) + [last]
    gather_both = gather_mat[0] + gather_mat[1]
    for j in range(chunks, last):
        outward(waiting.pop(0))
        each_peer(lambda q, j=j: give_back(j, me, q).wait_recv())
        inward(j, dot(gather_both, back[j]))
        waiting.append(j)
    for i in waiting:
        outward(i)

    for store in stores:
        store.wait()
    each_peer(lambda q: dispatch(0, q, me).wait_send())
    each_peer(lambda q: dispatch(1, q, me).wait_send())
    for i in range(last):
        each_peer(lambda q, i=i: give_back(i, q, me).wait_send())
    for i in range(last + 1):
        to_inner(i).wait_send()

    @pl.when(has_outer)
    def _():
        for i in range(last + 1):
            to_outer(i).wait_send()


def weight_grad_kernel(
    rows_t_ref,
    rows_grad_ref,
    hidden_t_ref,
    gate_ref,
    up_ref,
    mixed_ref,
    tokens_grad_ref,
    combine_ref,
    gate_out,
    up_out,
    down_out,
    mixed_out,
    tokens_grad_out,
    combine_out,
):
    mixed_out[...] = mixed_ref[...]
    tokens_grad_out[...] = tokens_grad_ref[...]
    combine_out[...] = combine_ref[...]
    gate_out[...] = dot(rows_t_ref[...], gate_ref[...]).astype(BF16)
    up_out[...] = dot(rows_t_ref[...], up_ref[...]).astype(BF16)
    down_out[...] = dot(hidden_t_ref[...], rows_grad_ref[...]).astype(BF16)


def weight_grads(rows_t, rows_grad, hidden_t, gate_grad, up_grad, mixed, tokens_grad, combine):
    places, features = rows_grad.shape
    units = gate_grad.shape[1]
    block = 256
    tall = pl.BlockSpec((block, units), lambda i: (i, 0))
    wide = pl.BlockSpec((units, block), lambda i: (0, i))
    whole = pl.BlockSpec((places, units), lambda i: (0, 0))
    token_count = mixed.shape[0]
    token_cols = pl.BlockSpec((token_count, block), lambda i: (0, i))
    pair_sums = pl.BlockSpec((2, token_count), lambda i: (0, 0))
    return pl.pallas_call(
        weight_grad_kernel,
        grid=(features // block,),
        in_specs=[
            pl.BlockSpec((block, places), lambda i: (i, 0)),
            pl.BlockSpec((places, block), lambda i: (0, i)),
            pl.BlockSpec((units, places), lambda i: (0, 0)),
            whole,
            whole,
            token_cols,
            token_cols,
            pair_sums,
        ],
        out_specs=[tall, tall, wide, token_cols, token_cols, pair_sums],
        out_shape=[
            jax.ShapeDtypeStruct((features, units), BF16),
            jax.ShapeDtypeStruct((features, units), BF16),
            jax.ShapeDtypeStruct((units, features), BF16),
            jax.ShapeDtypeStruct((token_count, features), BF16),
            jax.ShapeDtypeStruct((token_count, features), BF16),
            jax.ShapeDtypeStruct((2, token_count), F32),
        ],
        compiler_params=pltpu.CompilerParams(vmem_limit_bytes=60 << 20),
        cost_estimate=pl.CostEstimate(
            flops=6 * places * features * units,
            bytes_accessed=6 * features * units + 4 * places * features + 6 * places * units,
            transcendentals=0,
        ),
    )(rows_t, rows_grad, hidden_t, gate_grad, up_grad, mixed, tokens_grad, combine)


def shards(experts, lines, tokens, out_grad, routes, combine_weights, w_gate, w_up, w_down):
    token_count, features = tokens.shape
    units = w_gate.shape[2]
    cap = token_count // 4
    places = experts * cap
    chunks = features // CHUNK
    vmem = pl.BlockSpec(memory_space=pltpu.VMEM)
    hbm = pl.BlockSpec(memory_space=pl.ANY)
    dma = pltpu.SemaphoreType.DMA
    outs = pl.pallas_call(
        functools.partial(layer_kernel, experts, lines),
        in_specs=[vmem] * 4 + [hbm] * 3,
        out_specs=[vmem] * 3 + [hbm] * 5,
        out_shape=[
            jax.ShapeDtypeStruct((token_count, features), BF16),
            jax.ShapeDtypeStruct((token_count, features), BF16),
            jax.ShapeDtypeStruct((2, token_count), F32),
            jax.ShapeDtypeStruct((features, places), BF16),
            jax.ShapeDtypeStruct((places, features), BF16),
            jax.ShapeDtypeStruct((units, places), BF16),
            jax.ShapeDtypeStruct((places, units), BF16),
            jax.ShapeDtypeStruct((places, units), BF16),
        ],
        scratch_shapes=[
            pltpu.VMEM((features, units), BF16),
            pltpu.VMEM((features, units), BF16),
            pltpu.VMEM((units, features), BF16),
            pltpu.VMEM((2, places, features), BF16),
            pltpu.VMEM((2, places, features), BF16),
            pltpu.VMEM((places, units), F32),
            pltpu.VMEM((places, units), F32),
            pltpu.VMEM((places, units), BF16),
            pltpu.VMEM((places, units), BF16),
            pltpu.VMEM((places, units), BF16),
            pltpu.VMEM((features, places), BF16),
            pltpu.VMEM((units, places), BF16),
            pltpu.VMEM((2, token_count, places), BF16),
            pltpu.VMEM((2 * chunks, places, CHUNK), BF16),
            pltpu.VMEM((2 * chunks, places, CHUNK), BF16),
            pltpu.VMEM((2 * chunks, token_count, CHUNK), BF16),
            pltpu.VMEM((2, 2 * chunks, token_count, CHUNK), BF16),
            pltpu.VMEM((2 * chunks, token_count, CHUNK), BF16),
            pltpu.VMEM((8, token_count), F32),
            pltpu.VMEM((2, 8, token_count), F32),
            pltpu.VMEM((8, token_count), F32),
            dma((3,)),
            dma((5,)),
            dma((2, experts)),
            dma((2, experts)),
            dma((2 * chunks, experts)),
            dma((2 * chunks, experts)),
            dma((2 * chunks + 1,)),
            dma((2, 2 * chunks + 1)),
            dma((2 * chunks + 1,)),
        ],
        compiler_params=pltpu.CompilerParams(
            collective_id=0, has_side_effects=True, vmem_limit_bytes=56 << 20
        ),
        cost_estimate=pl.CostEstimate(
            flops=12 * places * features * units,
            bytes_accessed=6 * features * units,
            transcendentals=2 * places * units,
        ),
    )(tokens, out_grad, routes.T, combine_weights.T, w_gate[0], w_up[0], w_down[0])
    mixed, tokens_grad, combine, rows_t, rows_grad, hidden_t, gate_grad, up_grad = outs
    gate_wg, up_wg, down_wg, mixed, tokens_grad, combine = weight_grads(
        rows_t, rows_grad, hidden_t, gate_grad, up_grad, mixed, tokens_grad, combine
    )
    return mixed, tokens_grad, combine.T, gate_wg[None], up_wg[None], down_wg[None]


def solution(mesh):
    rows = P("expert", None)
    columns = P("expert", None, "etp")
    return jax.shard_map(
        functools.partial(shards, mesh.shape["expert"], mesh.shape["etp"]),
        mesh=mesh,
        in_specs=(rows, rows, rows, rows, columns, columns, P("expert", "etp", None)),
        out_specs=(rows, rows, rows, columns, columns, P("expert", "etp", None)),
        check_vma=False,
    )
```

```python
import functools

import jax
import jax.numpy as jnp
from jax import lax
from jax.experimental import pallas as pl
from jax.experimental.pallas import tpu as pltpu
from jax.sharding import PartitionSpec as P

MESH = pl.DeviceIdType.MESH
BF16 = jnp.bfloat16
F32 = jnp.float32
CHUNK = 512
LANES = 128
LAG = 2
STEP = 256


def dot(left, right):
    return jnp.dot(left, right, preferred_element_type=F32)


def contract_last(left, right):
    return lax.dot_general(left, right, (((1,), (1,)), ((), ())), preferred_element_type=F32)


def contract_first(left, right):
    return lax.dot_general(left, right, (((0,), (0,)), ((), ())), preferred_element_type=F32)


def one_hot_places(routes_row, routes_col, cap, places):
    tokens = routes_row.shape[1]
    before_by = lax.broadcasted_iota(jnp.int32, (tokens, tokens), 0)
    before_at = lax.broadcasted_iota(jnp.int32, (tokens, tokens), 1)
    upper = (before_by < before_at).astype(F32).astype(BF16)
    lower = (before_by > before_at).astype(F32).astype(BF16)
    expert_down = lax.broadcasted_iota(jnp.int32, (LANES, tokens), 0)
    expert_across = lax.broadcasted_iota(jnp.int32, (tokens, LANES), 1)
    named_down = [(expert_down == routes_row[k : k + 1, :]).astype(F32) for k in range(2)]
    named_across = [
        (expert_across.astype(F32) == routes_col[:, k : k + 1]).astype(F32) for k in range(2)
    ]
    earlier_down = dot((named_down[0] + named_down[1]).astype(BF16), upper)
    earlier_across = dot(lower, (named_across[0] + named_across[1]).astype(BF16))
    start_down = earlier_down + expert_down.astype(F32) * cap
    start_across = earlier_across + expert_across.astype(F32) * cap
    place_down = lax.broadcasted_iota(jnp.int32, (places, tokens), 0).astype(F32)
    place_across = lax.broadcasted_iota(jnp.int32, (tokens, places), 1).astype(F32)
    scatter, gather = [], []
    for k in range(2):
        row = jnp.sum(named_down[k] * start_down, axis=0, keepdims=True)
        col = jnp.sum(named_across[k] * start_across, axis=1, keepdims=True)
        scatter.append((place_down == row).astype(F32).astype(BF16))
        gather.append((place_across == col).astype(F32).astype(BF16))
    return scatter, gather


def layer_kernel(
    experts,
    lines,
    tokens_ref,
    grad_ref,
    routes_ref,
    weights_ref,
    gate_hbm,
    up_hbm,
    down_hbm,
    total_ref,
    combine_ref,
    rows_out,
    hidden_out,
    pre_grad_out,
    both_w,
    down_w,
    send,
    rows,
    pre,
    hidden,
    pre_grad,
    scatter_mat,
    gather_mat,
    weight_cols,
    products,
    part,
    back,
    line_own,
    line_in,
    dot_own,
    dot_in,
    dot_total,
    load_sem,
    store_sem,
    send_sem,
    recv_sem,
    part_sem,
    back_sem,
    inner_sem,
    line_sem,
    outer_sem,
):
    token_count, features = tokens_ref.shape
    cap = token_count // 4
    places = experts * cap
    chunks = features // CHUNK
    last = 2 * chunks
    strips = hidden.shape[1] // LANES
    me = lax.axis_index("expert")
    z = lax.axis_index("etp")
    half = lines // 2
    side = 1 - z // half
    inner = z + 2 * side - 1
    outer = z - 2 * side + 1
    has_outer = jnp.logical_and(z > 0, z < lines - 1)
    center = jnp.logical_or(z == half - 1, z == half)
    kind = jnp.where(center, 1, 0)

    def strip(n, width):
        return pl.ds(pl.multiple_of(n * width, width), width)

    def load(i, n):
        source = (gate_hbm, up_hbm)[i]
        return pltpu.make_async_copy(
            source.at[:, strip(n, LANES)],
            both_w.at[:, strip(2 * n + i, LANES)],
            load_sem.at[2 * n + i],
        )

    def loop(count, start=0):
        return lambda body: lax.fori_loop(start, count, lambda i, c: (body(i), c)[1], 0)

    load_down = pltpu.make_async_copy(down_hbm, down_w, load_sem.at[2 * strips])

    @loop(strips)
    def _(n):
        load(0, n).start()
        load(1, n).start()

    load_down.start()

    barrier = pltpu.get_barrier_semaphore()

    def each_peer(action):
        loop(experts, 1)(lambda d: action(lax.rem(me + d, experts)))

    @each_peer
    def _(peer):
        pl.semaphore_signal(barrier, inc=1, device_id={"expert": peer}, device_id_type=MESH)

    pl.semaphore_signal(barrier, inc=1, device_id={"etp": inner}, device_id_type=MESH)

    @pl.when(has_outer)
    def _():
        pl.semaphore_signal(barrier, inc=1, device_id={"etp": outer}, device_id_type=MESH)

    def block_of(index):
        return strip(index, cap)

    mine = block_of(me)

    def dispatch(i, peer, owner):
        return pltpu.make_async_remote_copy(
            src_ref=send.at[i, block_of(peer)],
            dst_ref=rows.at[i, block_of(owner)],
            send_sem=send_sem.at[i, peer],
            recv_sem=recv_sem.at[i, owner],
            device_id={"expert": peer},
            device_id_type=MESH,
        )

    def give_back(i, peer, owner):
        return pltpu.make_async_remote_copy(
            src_ref=part.at[i, block_of(peer)],
            dst_ref=back.at[i, block_of(owner)],
            send_sem=part_sem.at[i, peer],
            recv_sem=back_sem.at[i, owner],
            device_id={"expert": peer},
            device_id_type=MESH,
        )

    sub = lax.broadcasted_iota(jnp.int32, (LANES, token_count), 0)
    table = jnp.where(sub == 0, routes_ref[0:1, :], routes_ref[1:2, :]).astype(F32)
    table = jnp.where(sub == 2, weights_ref[0:1, :], table)
    table = jnp.where(sub == 3, weights_ref[1:2, :], table).T
    scatter, gather = one_hot_places(routes_ref[...], table, cap, places)
    for k in range(2):
        scatter_mat[k] = scatter[k]
        gather_mat[k] = gather[k]
        weight_cols[k] = jnp.broadcast_to(table[:, 2 + k : 3 + k], (token_count, LANES))
    products[...] = jnp.zeros_like(products)
    scatter_mat[2] = scatter[0] + scatter[1]
    gather_mat[2] = gather[0] + gather[1]

    @loop(features // STEP)
    def _(c):
        cols = strip(c, STEP)
        send[0, :, cols] = dot(scatter_mat[2], tokens_ref[:, cols]).astype(BF16)

    pl.semaphore_wait(barrier, experts + jnp.where(has_outer, 1, 0))
    each_peer(lambda q: dispatch(0, q, me).start())
    rows[0, mine] = send[0, mine]

    @loop(features // STEP)
    def _(c):
        cols = strip(c, STEP)
        value = grad_ref[:, cols].astype(F32)
        scaled = [(weight_cols[k][:, :1] * value).astype(BF16) for k in range(2)]
        send[1, :, cols] = (dot(scatter_mat[0], scaled[0]) + dot(scatter_mat[1], scaled[1])).astype(
            BF16
        )

    each_peer(lambda q: dispatch(1, q, me).start())
    rows[1, mine] = send[1, mine]

    @loop(strips)
    def _(n):
        load(0, n).wait()
        load(1, n).wait()

    load_down.wait()
    each_peer(lambda q: dispatch(0, me, q).wait_recv())

    @loop(strips)
    def _(n):
        both = strip(n, 2 * LANES)
        value = dot(rows[0], both_w[:, both])
        pre[:, both] = value
        gate_value = value[:, :LANES]
        hidden[:, strip(n, LANES)] = (
            gate_value * jax.nn.sigmoid(gate_value) * value[:, LANES:]
        ).astype(BF16)

    def send_back(i):
        each_peer(lambda q: give_back(i, q, me).start())
        back[i, mine] = part[i, mine]

    @loop(chunks)
    def _(c):
        part[c] = dot(hidden[...], down_w[:, strip(c, CHUNK)]).astype(BF16)
        send_back(c)

    each_peer(lambda q: dispatch(1, me, q).wait_recv())

    @loop(strips)
    def _(n):
        both = strip(n, 2 * LANES)
        hidden_grad = contract_last(rows[1], down_w[strip(n, LANES), :])
        value = pre[:, both]
        gate_value, up_value = value[:, :LANES], value[:, LANES:]
        sig = jax.nn.sigmoid(gate_value)
        pre_grad[:, strip(2 * n, LANES)] = (
            hidden_grad * up_value * sig * (1.0 + gate_value * (1.0 - sig))
        ).astype(BF16)
        pre_grad[:, strip(2 * n + 1, LANES)] = (hidden_grad * (gate_value * sig)).astype(BF16)

    stores = [
        pltpu.make_async_copy(src, dst, store_sem.at[i])
        for i, (src, dst) in enumerate(
            ((rows, rows_out), (hidden, hidden_out), (pre_grad, pre_grad_out))
        )
    ]
    for store in stores:
        store.start()

    def line_copy(i, source, where, target, send_line, peer):
        is_dot = isinstance(i, int)
        return pltpu.make_async_remote_copy(
            src_ref=source,
            dst_ref=dot_in.at[where] if is_dot else line_in.at[where, i],
            send_sem=send_line.at[i],
            recv_sem=line_sem.at[target, i],
            device_id={"etp": peer},
            device_id_type=MESH,
        )

    def own_of(i):
        return dot_own if isinstance(i, int) else line_own.at[i]

    def total_of(i):
        return dot_total if isinstance(i, int) else total_ref.at[i]

    def came(i, where):
        return dot_in.at[where] if isinstance(i, int) else line_in.at[where, i]

    def to_inner(i):
        return line_copy(i, own_of(i), kind, kind, inner_sem, inner)

    def to_outer(i):
        return line_copy(i, total_of(i), 1, 1, outer_sem, outer)

    def arrived(i, where):
        return line_copy(i, own_of(i), where, where, inner_sem, inner)

    def inward(i, value):
        own = own_of(i)

        @pl.when(has_outer)
        def _():
            arrived(i, 0).wait_recv()
            own[...] = (value + came(i, 0)[...].astype(F32)).astype(own.dtype)

        @pl.when(jnp.logical_not(has_outer))
        def _():
            own[...] = value.astype(own.dtype)

        to_inner(i).start()

    def outward(i):
        own, total = own_of(i), total_of(i)
        arrived(i, 1).wait_recv()

        @pl.when(center)
        def _():
            total[...] = (own[...].astype(F32) + came(i, 1)[...].astype(F32)).astype(own.dtype)

        @pl.when(jnp.logical_not(center))
        def _():
            total[...] = came(i, 1)[...]

        @pl.when(has_outer)
        def _():
            to_outer(i).start()

    @loop(chunks)
    def _(i):
        j = chunks + i
        cols = strip(i, CHUNK)
        part[j] = contract_last(pre_grad[...], both_w[cols, :]).astype(BF16)
        send_back(j)
        each_peer(lambda q: give_back(i, me, q).wait_recv())
        pairs = [dot(gather_mat[k], back[i]) for k in range(2)]
        value = grad_ref[:, cols].astype(F32)
        for k in range(2):
            term = value * pairs[k]
            products[k] += sum(
                term[:, s * LANES : (s + 1) * LANES] for s in range(CHUNK // LANES)
            )
        inward(i, weight_cols[0][:, :1] * pairs[0] + weight_cols[1][:, :1] * pairs[1])

        @pl.when(i >= LAG)
        def _():
            outward(i - LAG)

    sums = [jnp.sum(products[k], axis=1, keepdims=True) for k in range(2)]
    lane = lax.broadcasted_iota(jnp.int32, (token_count, LANES), 1)
    inward(last, jnp.where(lane == 0, sums[0], jnp.where(lane == 1, sums[1], 0.0)).T[:8])

    @loop(last, chunks)
    def _(j):
        outward(j - LAG)
        each_peer(lambda q: give_back(j, me, q).wait_recv())
        inward(j, dot(gather_mat[2], back[j]))

    outward(last)
    combine_ref[...] = dot_total[:2]
    loop(last, last - LAG)(outward)

    for store in stores:
        store.wait()

    @each_peer
    def _(q):
        dispatch(0, q, me).wait_send()
        dispatch(1, q, me).wait_send()
        loop(last)(lambda i: give_back(i, q, me).wait_send())

    loop(last)(lambda i: to_inner(i).wait_send())
    to_inner(last).wait_send()

    @pl.when(has_outer)
    def _():
        loop(last)(lambda i: to_outer(i).wait_send())
        to_outer(last).wait_send()


def weight_grad_kernel(
    rows_ref,
    rows_grad_ref,
    hidden_ref,
    pre_grad_ref,
    mixed_ref,
    tokens_grad_ref,
    combine_ref,
    gate_out,
    up_out,
    down_out,
    mixed_out,
    tokens_grad_out,
    combine_out,
    hidden_t,
    rows_t,
):
    strips = hidden_ref.shape[1] // LANES

    def strip(n, width):
        return pl.ds(pl.multiple_of(n * width, width), width)

    def turn(n, carry):
        hidden_t[strip(n, LANES), :] = hidden_ref[:, strip(n, LANES)].T
        return carry

    @pl.when(pl.program_id(0) == 0)
    def _():
        lax.fori_loop(0, strips, turn, 0)

    mixed_out[...] = mixed_ref[0]
    tokens_grad_out[...] = tokens_grad_ref[0]
    combine_out[...] = combine_ref[...]
    rows_t[...] = rows_ref[0].T

    def step(n, carry):
        one = strip(n, LANES)
        both = dot(rows_t[...], pre_grad_ref[:, strip(n, 2 * LANES)]).astype(BF16)
        gate_out[:, one] = both[:, :LANES]
        up_out[:, one] = both[:, LANES:]
        down_out[one, :] = dot(hidden_t[one, :], rows_grad_ref[0]).astype(BF16)
        return carry

    lax.fori_loop(0, strips, step, 0)


def weight_grads(rows, hidden, pre_grad, total, combine):
    _, places, features = rows.shape
    units = hidden.shape[1]
    chunks, token_count = total.shape[0] // 2, total.shape[1]
    split = CHUNK // STEP
    tall = pl.BlockSpec((STEP, units), lambda i: (i, 0))
    wide = pl.BlockSpec((units, STEP), lambda i: (0, i))
    token_cols = pl.BlockSpec((token_count, STEP), lambda i: (0, i))
    pair_sums = pl.BlockSpec((2, token_count), lambda i: (0, 0))
    return pl.pallas_call(
        weight_grad_kernel,
        grid=(features // STEP,),
        in_specs=[
            pl.BlockSpec((1, places, STEP), lambda i: (0, 0, i)),
            pl.BlockSpec((1, places, STEP), lambda i: (1, 0, i)),
            pl.BlockSpec((places, units), lambda i: (0, 0)),
            pl.BlockSpec((places, 2 * units), lambda i: (0, 0)),
            pl.BlockSpec((1, token_count, STEP), lambda i: (i // split, 0, i % split)),
            pl.BlockSpec((1, token_count, STEP), lambda i: (chunks + i // split, 0, i % split)),
            pair_sums,
        ],
        out_specs=[tall, tall, wide, token_cols, token_cols, pair_sums],
        out_shape=[
            jax.ShapeDtypeStruct((features, units), BF16),
            jax.ShapeDtypeStruct((features, units), BF16),
            jax.ShapeDtypeStruct((units, features), BF16),
            jax.ShapeDtypeStruct((token_count, features), BF16),
            jax.ShapeDtypeStruct((token_count, features), BF16),
            jax.ShapeDtypeStruct((2, token_count), F32),
        ],
        scratch_shapes=[pltpu.VMEM((units, places), BF16), pltpu.VMEM((STEP, places), BF16)],
        compiler_params=pltpu.CompilerParams(vmem_limit_bytes=60 << 20),
        cost_estimate=pl.CostEstimate(
            flops=6 * places * features * units,
            bytes_accessed=6 * features * units + 4 * places * features + 6 * places * units,
            transcendentals=0,
        ),
    )(rows, rows, hidden, pre_grad, total, total, combine)


def shards(experts, lines, tokens, out_grad, routes, combine_weights, w_gate, w_up, w_down):
    token_count, features = tokens.shape
    units = w_gate.shape[2]
    cap = token_count // 4
    places = experts * cap
    chunks = features // CHUNK
    items = 2 * chunks
    vmem = pl.BlockSpec(memory_space=pltpu.VMEM)
    hbm = pl.BlockSpec(memory_space=pl.ANY)
    dma = pltpu.SemaphoreType.DMA
    total, combine, rows, hidden, pre_grad = pl.pallas_call(
        functools.partial(layer_kernel, experts, lines),
        in_specs=[vmem] * 4 + [hbm] * 3,
        out_specs=[vmem] * 2 + [hbm] * 3,
        out_shape=[
            jax.ShapeDtypeStruct((items, token_count, CHUNK), BF16),
            jax.ShapeDtypeStruct((2, token_count), F32),
            jax.ShapeDtypeStruct((2, places, features), BF16),
            jax.ShapeDtypeStruct((places, units), BF16),
            jax.ShapeDtypeStruct((places, 2 * units), BF16),
        ],
        scratch_shapes=[
            pltpu.VMEM((features, 2 * units), BF16),
            pltpu.VMEM((units, features), BF16),
            pltpu.VMEM((2, places, features), BF16),
            pltpu.VMEM((2, places, features), BF16),
            pltpu.VMEM((places, 2 * units), F32),
            pltpu.VMEM((places, units), BF16),
            pltpu.VMEM((places, 2 * units), BF16),
            pltpu.VMEM((3, places, token_count), BF16),
            pltpu.VMEM((3, token_count, places), BF16),
            pltpu.VMEM((2, token_count, LANES), F32),
            pltpu.VMEM((2, token_count, LANES), F32),
            pltpu.VMEM((items, places, CHUNK), BF16),
            pltpu.VMEM((items, places, CHUNK), BF16),
            pltpu.VMEM((items, token_count, CHUNK), BF16),
            pltpu.VMEM((2, items, token_count, CHUNK), BF16),
            pltpu.VMEM((8, token_count), F32),
            pltpu.VMEM((2, 8, token_count), F32),
            pltpu.VMEM((8, token_count), F32),
            dma((2 * (units // LANES) + 1,)),
            dma((3,)),
            dma((2, experts)),
            dma((2, experts)),
            dma((items, experts)),
            dma((items, experts)),
            dma((items + 1,)),
            dma((2, items + 1)),
            dma((items + 1,)),
        ],
        compiler_params=pltpu.CompilerParams(
            collective_id=0, has_side_effects=True, vmem_limit_bytes=56 << 20
        ),
        cost_estimate=pl.CostEstimate(
            flops=12 * places * features * units,
            bytes_accessed=6 * features * units,
            transcendentals=2 * places * units,
        ),
    )(tokens, out_grad, routes.T, combine_weights.T, w_gate[0], w_up[0], w_down[0])
    gate_wg, up_wg, down_wg, mixed, tokens_grad, combine = weight_grads(
        rows, hidden, pre_grad, total, combine
    )
    return mixed, tokens_grad, combine.T, gate_wg[None], up_wg[None], down_wg[None]


def solution(mesh):
    rows = P("expert", None)
    columns = P("expert", None, "etp")
    return jax.shard_map(
        functools.partial(shards, mesh.shape["expert"], mesh.shape["etp"]),
        mesh=mesh,
        in_specs=(rows, rows, rows, rows, columns, columns, P("expert", "etp", None)),
        out_specs=(rows, rows, rows, columns, columns, P("expert", "etp", None)),
        check_vma=False,
    )
```

```python
import functools

import jax
import jax.numpy as jnp
from jax import lax
from jax.experimental import pallas as pl
from jax.experimental.pallas import tpu as pltpu
from jax.sharding import PartitionSpec as P

MESH = pl.DeviceIdType.MESH
BF16 = jnp.bfloat16
F32 = jnp.float32
CHUNK = 1024
LANES = 128
LAG = 1
STEP = 256


def dot(left, right):
    return jnp.dot(left, right, preferred_element_type=F32)


def contract_last(left, right):
    return lax.dot_general(left, right, (((1,), (1,)), ((), ())), preferred_element_type=F32)


def contract_first(left, right):
    return lax.dot_general(left, right, (((0,), (0,)), ((), ())), preferred_element_type=F32)


def one_hot_places(routes_row, routes_col, cap, places):
    tokens = routes_row.shape[1]
    before_by = lax.broadcasted_iota(jnp.int32, (tokens, tokens), 0)
    before_at = lax.broadcasted_iota(jnp.int32, (tokens, tokens), 1)
    upper = (before_by < before_at).astype(F32).astype(BF16)
    lower = (before_by > before_at).astype(F32).astype(BF16)
    expert_down = lax.broadcasted_iota(jnp.int32, (LANES, tokens), 0)
    expert_across = lax.broadcasted_iota(jnp.int32, (tokens, LANES), 1)
    named_down = [(expert_down == routes_row[k : k + 1, :]).astype(F32) for k in range(2)]
    named_across = [
        (expert_across.astype(F32) == routes_col[:, k : k + 1]).astype(F32) for k in range(2)
    ]
    earlier_down = dot((named_down[0] + named_down[1]).astype(BF16), upper)
    earlier_across = dot(lower, (named_across[0] + named_across[1]).astype(BF16))
    start_down = earlier_down + expert_down.astype(F32) * cap
    start_across = earlier_across + expert_across.astype(F32) * cap
    place_down = lax.broadcasted_iota(jnp.int32, (places, tokens), 0).astype(F32)
    place_across = lax.broadcasted_iota(jnp.int32, (tokens, places), 1).astype(F32)
    scatter, gather = [], []
    for k in range(2):
        row = jnp.sum(named_down[k] * start_down, axis=0, keepdims=True)
        col = jnp.sum(named_across[k] * start_across, axis=1, keepdims=True)
        scatter.append((place_down == row).astype(F32).astype(BF16))
        gather.append((place_across == col).astype(F32).astype(BF16))
    return scatter, gather


def layer_kernel(
    experts,
    lines,
    tokens_ref,
    grad_ref,
    routes_ref,
    weights_ref,
    gate_hbm,
    up_hbm,
    down_hbm,
    total_ref,
    combine_ref,
    rows_out,
    hidden_out,
    pre_grad_out,
    both_w,
    down_w,
    send,
    rows,
    pre,
    hidden,
    pre_grad,
    scatter_mat,
    gather_mat,
    weight_cols,
    products,
    part,
    back,
    line_own,
    line_in,
    dot_own,
    dot_in,
    dot_total,
    load_sem,
    store_sem,
    send_sem,
    recv_sem,
    part_sem,
    back_sem,
    inner_sem,
    line_sem,
    outer_sem,
):
    token_count, features = tokens_ref.shape
    cap = token_count // 4
    places = experts * cap
    chunks = features // CHUNK
    last = 2 * chunks
    strips = hidden.shape[1] // LANES
    me = lax.axis_index("expert")
    z = lax.axis_index("etp")
    half = lines // 2
    side = 1 - z // half
    inner = z + 2 * side - 1
    outer = z - 2 * side + 1
    has_outer = jnp.logical_and(z > 0, z < lines - 1)
    center = jnp.logical_or(z == half - 1, z == half)
    kind = jnp.where(center, 1, 0)

    def strip(n, width):
        return pl.ds(pl.multiple_of(n * width, width), width)

    def load(i, n):
        source = (gate_hbm, up_hbm)[i]
        return pltpu.make_async_copy(
            source.at[:, strip(n, LANES)],
            both_w.at[:, strip(2 * n + i, LANES)],
            load_sem.at[2 * n + i],
        )

    def loop(count, start=0):
        return lambda body: lax.fori_loop(start, count, lambda i, c: (body(i), c)[1], 0)

    load_down = pltpu.make_async_copy(down_hbm, down_w, load_sem.at[2 * strips])

    @loop(strips)
    def _(n):
        load(0, n).start()
        load(1, n).start()

    load_down.start()

    barrier = pltpu.get_barrier_semaphore()

    def each_peer(action):
        loop(experts, 1)(lambda d: action(lax.rem(me + d, experts)))

    @each_peer
    def _(peer):
        pl.semaphore_signal(barrier, inc=1, device_id={"expert": peer}, device_id_type=MESH)

    pl.semaphore_signal(barrier, inc=1, device_id={"etp": inner}, device_id_type=MESH)

    @pl.when(has_outer)
    def _():
        pl.semaphore_signal(barrier, inc=1, device_id={"etp": outer}, device_id_type=MESH)

    def block_of(index):
        return strip(index, cap)

    mine = block_of(me)

    def dispatch(i, peer, owner):
        return pltpu.make_async_remote_copy(
            src_ref=send.at[i, block_of(peer)],
            dst_ref=rows.at[i, block_of(owner)],
            send_sem=send_sem.at[i, peer],
            recv_sem=recv_sem.at[i, owner],
            device_id={"expert": peer},
            device_id_type=MESH,
        )

    def give_back(i, peer, owner):
        return pltpu.make_async_remote_copy(
            src_ref=part.at[i, block_of(peer)],
            dst_ref=back.at[i, block_of(owner)],
            send_sem=part_sem.at[i, peer],
            recv_sem=back_sem.at[i, owner],
            device_id={"expert": peer},
            device_id_type=MESH,
        )

    sub = lax.broadcasted_iota(jnp.int32, (LANES, token_count), 0)
    table = jnp.where(sub == 0, routes_ref[0:1, :], routes_ref[1:2, :]).astype(F32)
    table = jnp.where(sub == 2, weights_ref[0:1, :], table)
    table = jnp.where(sub == 3, weights_ref[1:2, :], table).T
    scatter, gather = one_hot_places(routes_ref[...], table, cap, places)
    for k in range(2):
        scatter_mat[k] = scatter[k]
        gather_mat[k] = gather[k]
        weight_cols[k] = jnp.broadcast_to(table[:, 2 + k : 3 + k], (token_count, LANES))
    products[...] = jnp.zeros_like(products)
    scatter_mat[2] = scatter[0] + scatter[1]
    gather_mat[2] = gather[0] + gather[1]

    @loop(features // STEP)
    def _(c):
        cols = strip(c, STEP)
        send[0, :, cols] = dot(scatter_mat[2], tokens_ref[:, cols]).astype(BF16)

    pl.semaphore_wait(barrier, experts + jnp.where(has_outer, 1, 0))
    each_peer(lambda q: dispatch(0, q, me).start())
    rows[0, mine] = send[0, mine]

    @loop(features // STEP)
    def _(c):
        cols = strip(c, STEP)
        value = grad_ref[:, cols].astype(F32)
        scaled = [(weight_cols[k][:, :1] * value).astype(BF16) for k in range(2)]
        send[1, :, cols] = (dot(scatter_mat[0], scaled[0]) + dot(scatter_mat[1], scaled[1])).astype(
            BF16
        )

    each_peer(lambda q: dispatch(1, q, me).start())
    rows[1, mine] = send[1, mine]

    @loop(strips)
    def _(n):
        load(0, n).wait()
        load(1, n).wait()

    load_down.wait()
    each_peer(lambda q: dispatch(0, me, q).wait_recv())

    @loop(strips)
    def _(n):
        both = strip(n, 2 * LANES)
        value = dot(rows[0], both_w[:, both])
        pre[:, both] = value
        gate_value = value[:, :LANES]
        hidden[:, strip(n, LANES)] = (
            gate_value * jax.nn.sigmoid(gate_value) * value[:, LANES:]
        ).astype(BF16)

    def send_back(i):
        each_peer(lambda q: give_back(i, q, me).start())
        back[i, mine] = part[i, mine]

    @loop(chunks)
    def _(c):
        @loop(CHUNK // STEP)
        def _(n):
            cols = strip(c * (CHUNK // STEP) + n, STEP)
            part[c, :, strip(n, STEP)] = dot(hidden[...], down_w[:, cols]).astype(BF16)

        send_back(c)

    each_peer(lambda q: dispatch(1, me, q).wait_recv())

    @loop(strips)
    def _(n):
        both = strip(n, 2 * LANES)
        hidden_grad = contract_last(rows[1], down_w[strip(n, LANES), :])
        value = pre[:, both]
        gate_value, up_value = value[:, :LANES], value[:, LANES:]
        sig = jax.nn.sigmoid(gate_value)
        pre_grad[:, strip(2 * n, LANES)] = (
            hidden_grad * up_value * sig * (1.0 + gate_value * (1.0 - sig))
        ).astype(BF16)
        pre_grad[:, strip(2 * n + 1, LANES)] = (hidden_grad * (gate_value * sig)).astype(BF16)

    stores = [
        pltpu.make_async_copy(src, dst, store_sem.at[i])
        for i, (src, dst) in enumerate(
            ((rows, rows_out), (hidden, hidden_out), (pre_grad, pre_grad_out))
        )
    ]
    for store in stores:
        store.start()

    def line_copy(i, source, where, target, send_line, peer):
        is_dot = isinstance(i, int)
        return pltpu.make_async_remote_copy(
            src_ref=source,
            dst_ref=dot_in.at[where] if is_dot else line_in.at[where, i],
            send_sem=send_line.at[i],
            recv_sem=line_sem.at[target, i],
            device_id={"etp": peer},
            device_id_type=MESH,
        )

    def own_of(i):
        return dot_own if isinstance(i, int) else line_own.at[i]

    def total_of(i):
        return dot_total if isinstance(i, int) else total_ref.at[i]

    def came(i, where):
        return dot_in.at[where] if isinstance(i, int) else line_in.at[where, i]

    def to_inner(i):
        return line_copy(i, own_of(i), kind, kind, inner_sem, inner)

    def to_outer(i):
        return line_copy(i, total_of(i), 1, 1, outer_sem, outer)

    def arrived(i, where):
        return line_copy(i, own_of(i), where, where, inner_sem, inner)

    def inward(i, value):
        own = own_of(i)

        @pl.when(has_outer)
        def _():
            arrived(i, 0).wait_recv()
            own[...] = (value + came(i, 0)[...].astype(F32)).astype(own.dtype)

        @pl.when(jnp.logical_not(has_outer))
        def _():
            own[...] = value.astype(own.dtype)

        to_inner(i).start()

    def outward(i):
        own, total = own_of(i), total_of(i)
        arrived(i, 1).wait_recv()

        @pl.when(center)
        def _():
            total[...] = (own[...].astype(F32) + came(i, 1)[...].astype(F32)).astype(own.dtype)

        @pl.when(jnp.logical_not(center))
        def _():
            total[...] = came(i, 1)[...]

        @pl.when(has_outer)
        def _():
            to_outer(i).start()

    @loop(chunks)
    def _(i):
        @loop(CHUNK // STEP)
        def _(n):
            rows_of = strip(i * (CHUNK // STEP) + n, STEP)
            part[chunks + i, :, strip(n, STEP)] = contract_last(
                pre_grad[...], both_w[rows_of, :]
            ).astype(BF16)

        send_back(chunks + i)

    @loop(chunks)
    def _(i):
        cols = strip(i, CHUNK)
        each_peer(lambda q: give_back(i, me, q).wait_recv())
        pairs = [dot(gather_mat[k], back[i]) for k in range(2)]
        value = grad_ref[:, cols].astype(F32)
        for k in range(2):
            term = value * pairs[k]
            products[k] += sum(
                term[:, s * LANES : (s + 1) * LANES] for s in range(CHUNK // LANES)
            )
        inward(i, weight_cols[0][:, :1] * pairs[0] + weight_cols[1][:, :1] * pairs[1])

        @pl.when(i >= LAG)
        def _():
            outward(i - LAG)

    sums = [jnp.sum(products[k], axis=1, keepdims=True) for k in range(2)]
    lane = lax.broadcasted_iota(jnp.int32, (token_count, LANES), 1)
    inward(last, jnp.where(lane == 0, sums[0], jnp.where(lane == 1, sums[1], 0.0)).T[:8])

    @loop(last, chunks)
    def _(j):
        outward(j - LAG)
        each_peer(lambda q: give_back(j, me, q).wait_recv())
        inward(j, dot(gather_mat[2], back[j]))

    outward(last)
    combine_ref[...] = dot_total[:2]
    loop(last, last - LAG)(outward)

    for store in stores:
        store.wait()

    @each_peer
    def _(q):
        dispatch(0, q, me).wait_send()
        dispatch(1, q, me).wait_send()
        loop(last)(lambda i: give_back(i, q, me).wait_send())

    loop(last)(lambda i: to_inner(i).wait_send())
    to_inner(last).wait_send()

    @pl.when(has_outer)
    def _():
        loop(last)(lambda i: to_outer(i).wait_send())
        to_outer(last).wait_send()


def weight_grad_kernel(
    rows_hbm,
    hidden_hbm,
    pre_grad_hbm,
    total_hbm,
    combine_ref,
    gate_out,
    up_out,
    down_out,
    mixed_out,
    tokens_grad_out,
    combine_out,
    rows,
    hidden,
    pre_grad,
    hidden_t,
    gate_buf,
    up_buf,
    down_buf,
    load_sem,
    rows_sem,
    total_sem,
    store_sem,
):
    strips = hidden.shape[1] // LANES
    blocks = rows.shape[2] // STEP
    chunks = total_hbm.shape[0] // 2

    def strip(n, width):
        return pl.ds(pl.multiple_of(n * width, width), width)

    def load_rows(k, i):
        cols = strip(i, STEP)
        return pltpu.make_async_copy(
            rows_hbm.at[k, :, cols], rows.at[k, :, cols], rows_sem.at[k, i]
        )

    def store(i):
        cols = strip(i, STEP)
        pairs = (
            (gate_buf.at[cols, :], gate_out.at[cols, :]),
            (up_buf.at[cols, :], up_out.at[cols, :]),
            (down_buf.at[:, cols], down_out.at[:, cols]),
        )
        return [
            pltpu.make_async_copy(src, dst, store_sem.at[k, i])
            for k, (src, dst) in enumerate(pairs)
        ]

    loads = [
        pltpu.make_async_copy(hidden_hbm, hidden, load_sem.at[0]),
        pltpu.make_async_copy(pre_grad_hbm, pre_grad, load_sem.at[1]),
    ]
    for load in loads:
        load.start()

    def start_rows(i, carry):
        load_rows(0, i).start()
        load_rows(1, i).start()
        return carry

    lax.fori_loop(0, blocks, start_rows, 0)
    moves = [
        pltpu.make_async_copy(
            total_hbm.at[k * chunks + c],
            out.at[:, c * CHUNK : (c + 1) * CHUNK],
            total_sem.at[k * chunks + c],
        )
        for k, out in enumerate((mixed_out, tokens_grad_out))
        for c in range(chunks)
    ]
    for move in moves:
        move.start()
    combine_out[...] = combine_ref[...]
    for load in loads:
        load.wait()
    hidden_t[...] = hidden[...].T

    def step(i, carry):
        cols = strip(i, STEP)
        load_rows(0, i).wait()
        load_rows(1, i).wait()
        both = dot(rows[0, :, cols].T, pre_grad[...]).astype(BF16)
        for n in range(strips):
            one = slice(n * LANES, (n + 1) * LANES)
            gate_buf[cols, one] = both[:, 2 * n * LANES : (2 * n + 1) * LANES]
            up_buf[cols, one] = both[:, (2 * n + 1) * LANES : (2 * n + 2) * LANES]
        down_buf[:, cols] = dot(hidden_t[...], rows[1, :, cols]).astype(BF16)
        for copy in store(i):
            copy.start()
        return carry

    lax.fori_loop(0, blocks, step, 0)

    def finish(i, carry):
        for copy in store(i):
            copy.wait()
        return carry

    lax.fori_loop(0, blocks, finish, 0)
    for move in moves:
        move.wait()


def weight_grads(rows, hidden, pre_grad, total, combine):
    _, places, features = rows.shape
    units = hidden.shape[1]
    items, token_count, _ = total.shape
    blocks = features // STEP
    vmem = pl.BlockSpec(memory_space=pltpu.VMEM)
    hbm = pl.BlockSpec(memory_space=pl.ANY)
    dma = pltpu.SemaphoreType.DMA
    return pl.pallas_call(
        weight_grad_kernel,
        in_specs=[hbm] * 4 + [vmem],
        out_specs=[hbm] * 5 + [vmem],
        out_shape=[
            jax.ShapeDtypeStruct((features, units), BF16),
            jax.ShapeDtypeStruct((features, units), BF16),
            jax.ShapeDtypeStruct((units, features), BF16),
            jax.ShapeDtypeStruct((token_count, features), BF16),
            jax.ShapeDtypeStruct((token_count, features), BF16),
            jax.ShapeDtypeStruct((2, token_count), F32),
        ],
        scratch_shapes=[
            pltpu.VMEM((2, places, features), BF16),
            pltpu.VMEM((places, units), BF16),
            pltpu.VMEM((places, 2 * units), BF16),
            pltpu.VMEM((units, places), BF16),
            pltpu.VMEM((features, units), BF16),
            pltpu.VMEM((features, units), BF16),
            pltpu.VMEM((units, features), BF16),
            dma((2,)),
            dma((2, blocks)),
            dma((items,)),
            dma((3, blocks)),
        ],
        compiler_params=pltpu.CompilerParams(vmem_limit_bytes=60 << 20),
        cost_estimate=pl.CostEstimate(
            flops=6 * places * features * units,
            bytes_accessed=6 * features * units + 4 * places * features + 6 * places * units,
            transcendentals=0,
        ),
    )(rows, hidden, pre_grad, total, combine)


def shards(experts, lines, tokens, out_grad, routes, combine_weights, w_gate, w_up, w_down):
    token_count, features = tokens.shape
    units = w_gate.shape[2]
    cap = token_count // 4
    places = experts * cap
    chunks = features // CHUNK
    items = 2 * chunks
    vmem = pl.BlockSpec(memory_space=pltpu.VMEM)
    hbm = pl.BlockSpec(memory_space=pl.ANY)
    dma = pltpu.SemaphoreType.DMA
    total, combine, rows, hidden, pre_grad = pl.pallas_call(
        functools.partial(layer_kernel, experts, lines),
        in_specs=[vmem] * 4 + [hbm] * 3,
        out_specs=[vmem] * 2 + [hbm] * 3,
        out_shape=[
            jax.ShapeDtypeStruct((items, token_count, CHUNK), BF16),
            jax.ShapeDtypeStruct((2, token_count), F32),
            jax.ShapeDtypeStruct((2, places, features), BF16),
            jax.ShapeDtypeStruct((places, units), BF16),
            jax.ShapeDtypeStruct((places, 2 * units), BF16),
        ],
        scratch_shapes=[
            pltpu.VMEM((features, 2 * units), BF16),
            pltpu.VMEM((units, features), BF16),
            pltpu.VMEM((2, places, features), BF16),
            pltpu.VMEM((2, places, features), BF16),
            pltpu.VMEM((places, 2 * units), F32),
            pltpu.VMEM((places, units), BF16),
            pltpu.VMEM((places, 2 * units), BF16),
            pltpu.VMEM((3, places, token_count), BF16),
            pltpu.VMEM((3, token_count, places), BF16),
            pltpu.VMEM((2, token_count, LANES), F32),
            pltpu.VMEM((2, token_count, LANES), F32),
            pltpu.VMEM((items, places, CHUNK), BF16),
            pltpu.VMEM((items, places, CHUNK), BF16),
            pltpu.VMEM((items, token_count, CHUNK), BF16),
            pltpu.VMEM((2, items, token_count, CHUNK), BF16),
            pltpu.VMEM((8, token_count), F32),
            pltpu.VMEM((2, 8, token_count), F32),
            pltpu.VMEM((8, token_count), F32),
            dma((2 * (units // LANES) + 1,)),
            dma((3,)),
            dma((2, experts)),
            dma((2, experts)),
            dma((items, experts)),
            dma((items, experts)),
            dma((items + 1,)),
            dma((2, items + 1)),
            dma((items + 1,)),
        ],
        compiler_params=pltpu.CompilerParams(
            collective_id=0, has_side_effects=True, vmem_limit_bytes=56 << 20
        ),
        cost_estimate=pl.CostEstimate(
            flops=12 * places * features * units,
            bytes_accessed=6 * features * units,
            transcendentals=2 * places * units,
        ),
    )(tokens, out_grad, routes.T, combine_weights.T, w_gate[0], w_up[0], w_down[0])
    gate_wg, up_wg, down_wg, mixed, tokens_grad, combine = weight_grads(
        rows, hidden, pre_grad, total, combine
    )
    return mixed, tokens_grad, combine.T, gate_wg[None], up_wg[None], down_wg[None]


def solution(mesh):
    rows = P("expert", None)
    columns = P("expert", None, "etp")
    return jax.shard_map(
        functools.partial(shards, mesh.shape["expert"], mesh.shape["etp"]),
        mesh=mesh,
        in_specs=(rows, rows, rows, rows, columns, columns, P("expert", "etp", None)),
        out_specs=(rows, rows, rows, columns, columns, P("expert", "etp", None)),
        check_vma=False,
    )
```

```python
import functools

import jax
import jax.numpy as jnp
from jax import lax
from jax.experimental import pallas as pl
from jax.experimental.pallas import tpu as pltpu
from jax.sharding import PartitionSpec as P

MESH = pl.DeviceIdType.MESH
BF16 = jnp.bfloat16
F32 = jnp.float32
CHUNK = 1024
LANES = 128
LAG = 2
LINE = 512
SHARED = 3 / 8
STEP = 256


def dot(left, right):
    return jnp.dot(left, right, preferred_element_type=F32)


def contract_last(left, right):
    return lax.dot_general(left, right, (((1,), (1,)), ((), ())), preferred_element_type=F32)


def contract_first(left, right):
    return lax.dot_general(left, right, (((0,), (0,)), ((), ())), preferred_element_type=F32)


def one_hot_places(routes_row, routes_col, cap, places):
    tokens = routes_row.shape[1]
    before_by = lax.broadcasted_iota(jnp.int32, (tokens, tokens), 0)
    before_at = lax.broadcasted_iota(jnp.int32, (tokens, tokens), 1)
    upper = (before_by < before_at).astype(F32).astype(BF16)
    lower = (before_by > before_at).astype(F32).astype(BF16)
    expert_down = lax.broadcasted_iota(jnp.int32, (LANES, tokens), 0)
    expert_across = lax.broadcasted_iota(jnp.int32, (tokens, LANES), 1)
    named_down = [(expert_down == routes_row[k : k + 1, :]).astype(F32) for k in range(2)]
    named_across = [
        (expert_across.astype(F32) == routes_col[:, k : k + 1]).astype(F32) for k in range(2)
    ]
    earlier_down = dot((named_down[0] + named_down[1]).astype(BF16), upper)
    earlier_across = dot(lower, (named_across[0] + named_across[1]).astype(BF16))
    start_down = earlier_down + expert_down.astype(F32) * cap
    start_across = earlier_across + expert_across.astype(F32) * cap
    place_down = lax.broadcasted_iota(jnp.int32, (places, tokens), 0).astype(F32)
    place_across = lax.broadcasted_iota(jnp.int32, (tokens, places), 1).astype(F32)
    scatter, gather = [], []
    for k in range(2):
        row = jnp.sum(named_down[k] * start_down, axis=0, keepdims=True)
        col = jnp.sum(named_across[k] * start_across, axis=1, keepdims=True)
        scatter.append((place_down == row).astype(F32).astype(BF16))
        gather.append((place_across == col).astype(F32).astype(BF16))
    return scatter, gather


def layer_kernel(
    experts,
    lines,
    tokens_ref,
    grad_ref,
    routes_ref,
    weights_ref,
    gate_hbm,
    up_hbm,
    down_hbm,
    total_ref,
    combine_ref,
    rows_out,
    hidden_out,
    pre_grad_out,
    both_w,
    down_w,
    send,
    rows,
    pre,
    hidden,
    pre_grad,
    scatter_mat,
    gather_mat,
    weight_cols,
    products,
    part,
    back,
    line_own,
    line_in,
    dot_own,
    dot_in,
    dot_total,
    load_sem,
    store_sem,
    send_sem,
    recv_sem,
    pass_send_sem,
    pass_recv_sem,
    part_sem,
    back_sem,
    inner_sem,
    line_sem,
    outer_sem,
):
    token_count, features = tokens_ref.shape
    cap = token_count // 4
    places = experts * cap
    chunks = features // CHUNK
    items = 2 * chunks
    split = CHUNK // LINE
    last = items * split
    shared = int(features * SHARED) // LANES * LANES
    kept = features - shared
    strips = hidden.shape[1] // LANES
    me = lax.axis_index("expert")
    z = lax.axis_index("etp")
    half = lines // 2
    side = 1 - z // half
    inner = z + 2 * side - 1
    outer = z - 2 * side + 1
    has_outer = jnp.logical_and(z > 0, z < lines - 1)
    center = jnp.logical_or(z == half - 1, z == half)
    kind = jnp.where(center, 1, 0)
    parity = lax.rem(z, 2)
    partner = z + 1 - 2 * parity

    def strip(n, width):
        return pl.ds(pl.multiple_of(n * width, width), width)

    def load(i, n):
        source = (gate_hbm, up_hbm)[i]
        return pltpu.make_async_copy(
            source.at[:, strip(n, LANES)],
            both_w.at[:, strip(2 * n + i, LANES)],
            load_sem.at[2 * n + i],
        )

    def loop(count, start=0):
        return lambda body: lax.fori_loop(start, count, lambda i, c: (body(i), c)[1], 0)

    load_down = pltpu.make_async_copy(down_hbm, down_w, load_sem.at[2 * strips])

    @loop(strips)
    def _(n):
        load(0, n).start()
        load(1, n).start()

    load_down.start()

    barrier = pltpu.get_barrier_semaphore()

    def each_peer(action):
        loop(experts, 1)(lambda d: action(lax.rem(me + d, experts)))

    @each_peer
    def _(peer):
        pl.semaphore_signal(barrier, inc=1, device_id={"expert": peer}, device_id_type=MESH)

    pl.semaphore_signal(barrier, inc=1, device_id={"etp": inner}, device_id_type=MESH)

    @pl.when(has_outer)
    def _():
        pl.semaphore_signal(barrier, inc=1, device_id={"etp": outer}, device_id_type=MESH)

    def block_of(index):
        return strip(index, cap)

    mine = block_of(me)

    def dispatch(i, peer, owner):
        cols = pl.ds(pl.multiple_of(parity * shared, LANES), kept)
        return pltpu.make_async_remote_copy(
            src_ref=send.at[i, block_of(peer), cols],
            dst_ref=rows.at[i, block_of(owner), cols],
            send_sem=send_sem.at[i, peer],
            recv_sem=recv_sem.at[i, owner],
            device_id={"expert": peer},
            device_id_type=MESH,
        )

    def pass_on(i, owner, side_of):
        cols = pl.ds(pl.multiple_of(side_of * kept, LANES), shared)
        return pltpu.make_async_remote_copy(
            src_ref=rows.at[i, block_of(owner), cols],
            dst_ref=rows.at[i, block_of(owner), cols],
            send_sem=pass_send_sem.at[i, owner],
            recv_sem=pass_recv_sem.at[i, owner],
            device_id={"etp": partner},
            device_id_type=MESH,
        )

    def receive(i):
        def one(d):
            q = lax.rem(me + experts - d, experts)
            dispatch(i, me, q).wait_recv()
            pass_on(i, q, parity).start()

        loop(experts, 1)(one)

    def passed(i):
        each_peer(lambda q: pass_on(i, q, 1 - parity).wait_recv())

    def give_back(i, peer, owner):
        return pltpu.make_async_remote_copy(
            src_ref=part.at[i, block_of(peer)],
            dst_ref=back.at[i, block_of(owner)],
            send_sem=part_sem.at[i, peer],
            recv_sem=back_sem.at[i, owner],
            device_id={"expert": peer},
            device_id_type=MESH,
        )

    sub = lax.broadcasted_iota(jnp.int32, (LANES, token_count), 0)
    table = jnp.where(sub == 0, routes_ref[0:1, :], routes_ref[1:2, :]).astype(F32)
    table = jnp.where(sub == 2, weights_ref[0:1, :], table)
    table = jnp.where(sub == 3, weights_ref[1:2, :], table).T
    scatter, gather = one_hot_places(routes_ref[...], table, cap, places)
    for k in range(2):
        scatter_mat[k] = scatter[k]
        gather_mat[k] = gather[k]
        weight_cols[k] = jnp.broadcast_to(table[:, 2 + k : 3 + k], (token_count, LANES))
    products[...] = jnp.zeros_like(products)
    scatter_mat[2] = scatter[0] + scatter[1]
    gather_mat[2] = gather[0] + gather[1]

    @loop(features // STEP)
    def _(c):
        cols = strip(c, STEP)
        send[0, :, cols] = dot(scatter_mat[2], tokens_ref[:, cols]).astype(BF16)

    pl.semaphore_wait(barrier, experts + jnp.where(has_outer, 1, 0))
    each_peer(lambda q: dispatch(0, q, me).start())
    rows[0, mine] = send[0, mine]

    @loop(features // STEP)
    def _(c):
        cols = strip(c, STEP)
        value = grad_ref[:, cols].astype(F32)
        scaled = [(weight_cols[k][:, :1] * value).astype(BF16) for k in range(2)]
        send[1, :, cols] = (dot(scatter_mat[0], scaled[0]) + dot(scatter_mat[1], scaled[1])).astype(
            BF16
        )

    each_peer(lambda q: dispatch(1, q, me).start())
    rows[1, mine] = send[1, mine]

    @loop(strips)
    def _(n):
        load(0, n).wait()
        load(1, n).wait()

    load_down.wait()
    receive(0)
    passed(0)

    @loop(strips)
    def _(n):
        both = strip(n, 2 * LANES)
        value = dot(rows[0], both_w[:, both])
        pre[:, both] = value
        gate_value = value[:, :LANES]
        hidden[:, strip(n, LANES)] = (
            gate_value * jax.nn.sigmoid(gate_value) * value[:, LANES:]
        ).astype(BF16)

    receive(1)

    def send_back(i):
        each_peer(lambda q: give_back(i, q, me).start())
        back[i, mine] = part[i, mine]

    @loop(chunks)
    def _(c):
        @loop(CHUNK // STEP)
        def _(n):
            cols = strip(c * (CHUNK // STEP) + n, STEP)
            part[c, :, strip(n, STEP)] = dot(hidden[...], down_w[:, cols]).astype(BF16)

        send_back(c)

    passed(1)

    @loop(strips)
    def _(n):
        both = strip(n, 2 * LANES)
        hidden_grad = contract_last(rows[1], down_w[strip(n, LANES), :])
        value = pre[:, both]
        gate_value, up_value = value[:, :LANES], value[:, LANES:]
        sig = jax.nn.sigmoid(gate_value)
        pre_grad[:, strip(2 * n, LANES)] = (
            hidden_grad * up_value * sig * (1.0 + gate_value * (1.0 - sig))
        ).astype(BF16)
        pre_grad[:, strip(2 * n + 1, LANES)] = (hidden_grad * (gate_value * sig)).astype(BF16)

    stores = [
        pltpu.make_async_copy(src, dst, store_sem.at[i])
        for i, (src, dst) in enumerate(
            ((rows, rows_out), (hidden, hidden_out), (pre_grad, pre_grad_out))
        )
    ]
    for store in stores:
        store.start()

    def line_copy(i, source, where, target, send_line, peer):
        is_dot = isinstance(i, int)
        return pltpu.make_async_remote_copy(
            src_ref=source,
            dst_ref=dot_in.at[where] if is_dot else line_in.at[where, i],
            send_sem=send_line.at[i],
            recv_sem=line_sem.at[target, i],
            device_id={"etp": peer},
            device_id_type=MESH,
        )

    def own_of(i):
        return dot_own if isinstance(i, int) else line_own.at[i]

    def total_of(i):
        return dot_total if isinstance(i, int) else total_ref.at[i]

    def came(i, where):
        return dot_in.at[where] if isinstance(i, int) else line_in.at[where, i]

    def to_inner(i):
        return line_copy(i, own_of(i), kind, kind, inner_sem, inner)

    def to_outer(i):
        return line_copy(i, total_of(i), 1, 1, outer_sem, outer)

    def arrived(i, where):
        return line_copy(i, own_of(i), where, where, inner_sem, inner)

    def inward(i, value):
        own = own_of(i)

        @pl.when(has_outer)
        def _():
            arrived(i, 0).wait_recv()
            own[...] = (value + came(i, 0)[...].astype(F32)).astype(own.dtype)

        @pl.when(jnp.logical_not(has_outer))
        def _():
            own[...] = value.astype(own.dtype)

        to_inner(i).start()

    def outward(i):
        own, total = own_of(i), total_of(i)
        arrived(i, 1).wait_recv()

        @pl.when(center)
        def _():
            total[...] = (own[...].astype(F32) + came(i, 1)[...].astype(F32)).astype(own.dtype)

        @pl.when(jnp.logical_not(center))
        def _():
            total[...] = came(i, 1)[...]

        @pl.when(has_outer)
        def _():
            to_outer(i).start()

    @loop(chunks)
    def _(i):
        @loop(CHUNK // STEP)
        def _(n):
            rows_of = strip(i * (CHUNK // STEP) + n, STEP)
            part[chunks + i, :, strip(n, STEP)] = contract_last(
                pre_grad[...], both_w[rows_of, :]
            ).astype(BF16)

        send_back(chunks + i)

    @loop(chunks)
    def _(i):
        each_peer(lambda q: give_back(i, me, q).wait_recv())

        @loop(split)
        def _(n):
            at = i * split + n
            pairs = [dot(gather_mat[k], back[i, :, strip(n, LINE)]) for k in range(2)]
            value = grad_ref[:, strip(at, LINE)].astype(F32)
            for k in range(2):
                term = value * pairs[k]
                products[k] += sum(
                    term[:, s * LANES : (s + 1) * LANES] for s in range(LINE // LANES)
                )
            inward(at, weight_cols[0][:, :1] * pairs[0] + weight_cols[1][:, :1] * pairs[1])

            @pl.when(at >= LAG)
            def _():
                outward(at - LAG)

    sums = [jnp.sum(products[k], axis=1, keepdims=True) for k in range(2)]
    lane = lax.broadcasted_iota(jnp.int32, (token_count, LANES), 1)
    inward(last, jnp.where(lane == 0, sums[0], jnp.where(lane == 1, sums[1], 0.0)).T[:8])

    @loop(items, chunks)
    def _(j):
        each_peer(lambda q: give_back(j, me, q).wait_recv())

        @loop(split)
        def _(n):
            at = j * split + n
            outward(at - LAG)
            inward(at, dot(gather_mat[2], back[j, :, strip(n, LINE)]))

    outward(last)
    combine_ref[...] = dot_total[:2]
    loop(last, last - LAG)(outward)

    for store in stores:
        store.wait()

    @each_peer
    def _(q):
        dispatch(0, q, me).wait_send()
        dispatch(1, q, me).wait_send()
        pass_on(0, q, parity).wait_send()
        pass_on(1, q, parity).wait_send()
        loop(items)(lambda i: give_back(i, q, me).wait_send())

    loop(last)(lambda i: to_inner(i).wait_send())
    to_inner(last).wait_send()

    @pl.when(has_outer)
    def _():
        loop(last)(lambda i: to_outer(i).wait_send())
        to_outer(last).wait_send()


def weight_grad_kernel(
    rows_ref,
    rows_grad_ref,
    hidden_ref,
    pre_grad_ref,
    mixed_ref,
    tokens_grad_ref,
    combine_ref,
    gate_out,
    up_out,
    down_out,
    mixed_out,
    tokens_grad_out,
    combine_out,
    hidden_t,
    rows_t,
):
    strips = hidden_ref.shape[1] // LANES

    def strip(n, width):
        return pl.ds(pl.multiple_of(n * width, width), width)

    def turn(n, carry):
        hidden_t[strip(n, LANES), :] = hidden_ref[:, strip(n, LANES)].T
        return carry

    @pl.when(pl.program_id(0) == 0)
    def _():
        lax.fori_loop(0, strips, turn, 0)

    mixed_out[...] = mixed_ref[0]
    tokens_grad_out[...] = tokens_grad_ref[0]
    combine_out[...] = combine_ref[...]
    rows_t[...] = rows_ref[0].T

    both = dot(rows_t[...], pre_grad_ref[...]).astype(BF16)
    for n in range(strips):
        one = slice(n * LANES, (n + 1) * LANES)
        gate_out[:, one] = both[:, 2 * n * LANES : (2 * n + 1) * LANES]
        up_out[:, one] = both[:, (2 * n + 1) * LANES : (2 * n + 2) * LANES]
    down_out[...] = dot(hidden_t[...], rows_grad_ref[0]).astype(BF16)


def weight_grads(rows, hidden, pre_grad, total, combine):
    _, places, features = rows.shape
    units = hidden.shape[1]
    chunks, token_count = total.shape[0] // 2, total.shape[1]
    split = LINE // STEP
    tall = pl.BlockSpec((STEP, units), lambda i: (i, 0))
    wide = pl.BlockSpec((units, STEP), lambda i: (0, i))
    token_cols = pl.BlockSpec((token_count, STEP), lambda i: (0, i))
    pair_sums = pl.BlockSpec((2, token_count), lambda i: (0, 0))
    return pl.pallas_call(
        weight_grad_kernel,
        grid=(features // STEP,),
        in_specs=[
            pl.BlockSpec((1, places, STEP), lambda i: (0, 0, i)),
            pl.BlockSpec((1, places, STEP), lambda i: (1, 0, i)),
            pl.BlockSpec((places, units), lambda i: (0, 0)),
            pl.BlockSpec((places, 2 * units), lambda i: (0, 0)),
            pl.BlockSpec((1, token_count, STEP), lambda i: (i // split, 0, i % split)),
            pl.BlockSpec((1, token_count, STEP), lambda i: (chunks + i // split, 0, i % split)),
            pair_sums,
        ],
        out_specs=[tall, tall, wide, token_cols, token_cols, pair_sums],
        out_shape=[
            jax.ShapeDtypeStruct((features, units), BF16),
            jax.ShapeDtypeStruct((features, units), BF16),
            jax.ShapeDtypeStruct((units, features), BF16),
            jax.ShapeDtypeStruct((token_count, features), BF16),
            jax.ShapeDtypeStruct((token_count, features), BF16),
            jax.ShapeDtypeStruct((2, token_count), F32),
        ],
        scratch_shapes=[pltpu.VMEM((units, places), BF16), pltpu.VMEM((STEP, places), BF16)],
        compiler_params=pltpu.CompilerParams(vmem_limit_bytes=60 << 20),
        cost_estimate=pl.CostEstimate(
            flops=6 * places * features * units,
            bytes_accessed=6 * features * units + 4 * places * features + 6 * places * units,
            transcendentals=0,
        ),
    )(rows, rows, hidden, pre_grad, total, total, combine)


def shards(experts, lines, tokens, out_grad, routes, combine_weights, w_gate, w_up, w_down):
    token_count, features = tokens.shape
    units = w_gate.shape[2]
    cap = token_count // 4
    places = experts * cap
    chunks = features // CHUNK
    items = 2 * chunks
    line_items = items * CHUNK // LINE
    vmem = pl.BlockSpec(memory_space=pltpu.VMEM)
    hbm = pl.BlockSpec(memory_space=pl.ANY)
    dma = pltpu.SemaphoreType.DMA
    total, combine, rows, hidden, pre_grad = pl.pallas_call(
        functools.partial(layer_kernel, experts, lines),
        in_specs=[vmem] * 4 + [hbm] * 3,
        out_specs=[vmem] * 2 + [hbm] * 3,
        out_shape=[
            jax.ShapeDtypeStruct((line_items, token_count, LINE), BF16),
            jax.ShapeDtypeStruct((2, token_count), F32),
            jax.ShapeDtypeStruct((2, places, features), BF16),
            jax.ShapeDtypeStruct((places, units), BF16),
            jax.ShapeDtypeStruct((places, 2 * units), BF16),
        ],
        scratch_shapes=[
            pltpu.VMEM((features, 2 * units), BF16),
            pltpu.VMEM((units, features), BF16),
            pltpu.VMEM((2, places, features), BF16),
            pltpu.VMEM((2, places, features), BF16),
            pltpu.VMEM((places, 2 * units), F32),
            pltpu.VMEM((places, units), BF16),
            pltpu.VMEM((places, 2 * units), BF16),
            pltpu.VMEM((3, places, token_count), BF16),
            pltpu.VMEM((3, token_count, places), BF16),
            pltpu.VMEM((2, token_count, LANES), F32),
            pltpu.VMEM((2, token_count, LANES), F32),
            pltpu.VMEM((items, places, CHUNK), BF16),
            pltpu.VMEM((items, places, CHUNK), BF16),
            pltpu.VMEM((line_items, token_count, LINE), BF16),
            pltpu.VMEM((2, line_items, token_count, LINE), BF16),
            pltpu.VMEM((8, token_count), F32),
            pltpu.VMEM((2, 8, token_count), F32),
            pltpu.VMEM((8, token_count), F32),
            dma((2 * (units // LANES) + 1,)),
            dma((3,)),
            dma((2, experts)),
            dma((2, experts)),
            dma((2, experts)),
            dma((2, experts)),
            dma((items, experts)),
            dma((items, experts)),
            dma((line_items + 1,)),
            dma((2, line_items + 1)),
            dma((line_items + 1,)),
        ],
        compiler_params=pltpu.CompilerParams(
            collective_id=0, has_side_effects=True, vmem_limit_bytes=56 << 20
        ),
        cost_estimate=pl.CostEstimate(
            flops=12 * places * features * units,
            bytes_accessed=6 * features * units,
            transcendentals=2 * places * units,
        ),
    )(tokens, out_grad, routes.T, combine_weights.T, w_gate[0], w_up[0], w_down[0])
    gate_wg, up_wg, down_wg, mixed, tokens_grad, combine = weight_grads(
        rows, hidden, pre_grad, total, combine
    )
    return mixed, tokens_grad, combine.T, gate_wg[None], up_wg[None], down_wg[None]


def solution(mesh):
    rows = P("expert", None)
    columns = P("expert", None, "etp")
    return jax.shard_map(
        functools.partial(shards, mesh.shape["expert"], mesh.shape["etp"]),
        mesh=mesh,
        in_specs=(rows, rows, rows, rows, columns, columns, P("expert", "etp", None)),
        out_specs=(rows, rows, rows, columns, columns, P("expert", "etp", None)),
        check_vma=False,
    )
```

```python
import functools

import jax
import jax.numpy as jnp
from jax import lax
from jax.experimental import pallas as pl
from jax.experimental.pallas import tpu as pltpu
from jax.sharding import PartitionSpec as P

MESH = pl.DeviceIdType.MESH
BF16 = jnp.bfloat16
F32 = jnp.float32
CHUNK = 1024
LANES = 128
LAG = 3
LINE = 512
SHARED = 3 / 8
STEP = 256


def dot(left, right):
    return jnp.dot(left, right, preferred_element_type=F32)


def contract_last(left, right):
    return lax.dot_general(left, right, (((1,), (1,)), ((), ())), preferred_element_type=F32)


def contract_first(left, right):
    return lax.dot_general(left, right, (((0,), (0,)), ((), ())), preferred_element_type=F32)


def one_hot_places(routes_row, routes_col, cap, places):
    tokens = routes_row.shape[1]
    before_by = lax.broadcasted_iota(jnp.int32, (tokens, tokens), 0)
    before_at = lax.broadcasted_iota(jnp.int32, (tokens, tokens), 1)
    upper = (before_by < before_at).astype(F32).astype(BF16)
    lower = (before_by > before_at).astype(F32).astype(BF16)
    expert_down = lax.broadcasted_iota(jnp.int32, (LANES, tokens), 0)
    expert_across = lax.broadcasted_iota(jnp.int32, (tokens, LANES), 1)
    named_down = [(expert_down == routes_row[k : k + 1, :]).astype(F32) for k in range(2)]
    named_across = [
        (expert_across.astype(F32) == routes_col[:, k : k + 1]).astype(F32) for k in range(2)
    ]
    earlier_down = dot((named_down[0] + named_down[1]).astype(BF16), upper)
    earlier_across = dot(lower, (named_across[0] + named_across[1]).astype(BF16))
    start_down = earlier_down + expert_down.astype(F32) * cap
    start_across = earlier_across + expert_across.astype(F32) * cap
    place_down = lax.broadcasted_iota(jnp.int32, (places, tokens), 0).astype(F32)
    place_across = lax.broadcasted_iota(jnp.int32, (tokens, places), 1).astype(F32)
    scatter, gather = [], []
    for k in range(2):
        row = jnp.sum(named_down[k] * start_down, axis=0, keepdims=True)
        col = jnp.sum(named_across[k] * start_across, axis=1, keepdims=True)
        scatter.append((place_down == row).astype(F32).astype(BF16))
        gather.append((place_across == col).astype(F32).astype(BF16))
    return scatter, gather


def layer_kernel(
    experts,
    lines,
    tokens_ref,
    grad_ref,
    routes_ref,
    weights_ref,
    gate_hbm,
    up_hbm,
    down_hbm,
    total_ref,
    combine_ref,
    rows_out,
    hidden_out,
    pre_grad_out,
    both_w,
    down_w,
    send,
    rows,
    pre,
    hidden,
    pre_grad,
    scatter_mat,
    gather_mat,
    weight_cols,
    products,
    part,
    back,
    line_own,
    line_in,
    dot_own,
    dot_in,
    dot_total,
    load_sem,
    store_sem,
    send_sem,
    recv_sem,
    pass_send_sem,
    pass_recv_sem,
    part_sem,
    back_sem,
    inner_sem,
    line_sem,
    outer_sem,
):
    token_count, features = tokens_ref.shape
    cap = token_count // 4
    places = experts * cap
    chunks = features // CHUNK
    items = 2 * chunks
    split = CHUNK // LINE
    last = items * split
    shared = int(features * SHARED) // LANES * LANES
    kept = features - shared
    strips = hidden.shape[1] // LANES
    me = lax.axis_index("expert")
    z = lax.axis_index("etp")
    half = lines // 2
    side = 1 - z // half
    inner = z + 2 * side - 1
    outer = z - 2 * side + 1
    has_outer = jnp.logical_and(z > 0, z < lines - 1)
    center = jnp.logical_or(z == half - 1, z == half)
    kind = jnp.where(center, 1, 0)
    parity = lax.rem(z, 2)
    partner = z + 1 - 2 * parity

    def strip(n, width):
        return pl.ds(pl.multiple_of(n * width, width), width)

    def load(i, n):
        source = (gate_hbm, up_hbm)[i]
        return pltpu.make_async_copy(
            source.at[:, strip(n, LANES)],
            both_w.at[:, strip(2 * n + i, LANES)],
            load_sem.at[2 * n + i],
        )

    def loop(count, start=0):
        return lambda body: lax.fori_loop(start, count, lambda i, c: (body(i), c)[1], 0)

    load_down = pltpu.make_async_copy(down_hbm, down_w, load_sem.at[2 * strips])

    @loop(strips)
    def _(n):
        load(0, n).start()
        load(1, n).start()

    load_down.start()

    barrier = pltpu.get_barrier_semaphore()

    def each_peer(action):
        loop(experts, 1)(lambda d: action(lax.rem(me + d, experts)))

    @each_peer
    def _(peer):
        pl.semaphore_signal(barrier, inc=1, device_id={"expert": peer}, device_id_type=MESH)

    pl.semaphore_signal(barrier, inc=1, device_id={"etp": inner}, device_id_type=MESH)

    @pl.when(has_outer)
    def _():
        pl.semaphore_signal(barrier, inc=1, device_id={"etp": outer}, device_id_type=MESH)

    def block_of(index):
        return strip(index, cap)

    mine = block_of(me)

    def dispatch(i, peer, owner):
        cols = pl.ds(pl.multiple_of(parity * shared, LANES), kept)
        return pltpu.make_async_remote_copy(
            src_ref=send.at[i, block_of(peer), cols],
            dst_ref=rows.at[i, block_of(owner), cols],
            send_sem=send_sem.at[i, peer],
            recv_sem=recv_sem.at[i, owner],
            device_id={"expert": peer},
            device_id_type=MESH,
        )

    def pass_on(i, owner, side_of):
        cols = pl.ds(pl.multiple_of(side_of * kept, LANES), shared)
        return pltpu.make_async_remote_copy(
            src_ref=rows.at[i, block_of(owner), cols],
            dst_ref=rows.at[i, block_of(owner), cols],
            send_sem=pass_send_sem.at[i, owner],
            recv_sem=pass_recv_sem.at[i, owner],
            device_id={"etp": partner},
            device_id_type=MESH,
        )

    def receive(i):
        def one(d):
            q = lax.rem(me + experts - d, experts)
            dispatch(i, me, q).wait_recv()
            pass_on(i, q, parity).start()

        loop(experts, 1)(one)

    def passed(i):
        each_peer(lambda q: pass_on(i, q, 1 - parity).wait_recv())

    def give_back(i, peer, owner):
        return pltpu.make_async_remote_copy(
            src_ref=part.at[i, block_of(peer)],
            dst_ref=back.at[i, block_of(owner)],
            send_sem=part_sem.at[i, peer],
            recv_sem=back_sem.at[i, owner],
            device_id={"expert": peer},
            device_id_type=MESH,
        )

    sub = lax.broadcasted_iota(jnp.int32, (LANES, token_count), 0)
    table = jnp.where(sub == 0, routes_ref[0:1, :], routes_ref[1:2, :]).astype(F32)
    table = jnp.where(sub == 2, weights_ref[0:1, :], table)
    table = jnp.where(sub == 3, weights_ref[1:2, :], table).T
    scatter, gather = one_hot_places(routes_ref[...], table, cap, places)
    for k in range(2):
        scatter_mat[k] = scatter[k]
        gather_mat[k] = gather[k]
        weight_cols[k] = jnp.broadcast_to(table[:, 2 + k : 3 + k], (token_count, LANES))
    products[...] = jnp.zeros_like(products)
    scatter_mat[2] = scatter[0] + scatter[1]
    gather_mat[2] = gather[0] + gather[1]

    @loop(features // STEP)
    def _(c):
        cols = strip(c, STEP)
        send[0, :, cols] = dot(scatter_mat[2], tokens_ref[:, cols]).astype(BF16)

    pl.semaphore_wait(barrier, experts + jnp.where(has_outer, 1, 0))
    each_peer(lambda q: dispatch(0, q, me).start())
    rows[0, mine] = send[0, mine]

    @loop(features // STEP)
    def _(c):
        cols = strip(c, STEP)
        value = grad_ref[:, cols].astype(F32)
        scaled = [(weight_cols[k][:, :1] * value).astype(BF16) for k in range(2)]
        send[1, :, cols] = (dot(scatter_mat[0], scaled[0]) + dot(scatter_mat[1], scaled[1])).astype(
            BF16
        )

    each_peer(lambda q: dispatch(1, q, me).start())
    rows[1, mine] = send[1, mine]

    @loop(strips)
    def _(n):
        load(0, n).wait()
        load(1, n).wait()

    load_down.wait()
    receive(0)
    passed(0)

    @loop(strips)
    def _(n):
        both = strip(n, 2 * LANES)
        value = dot(rows[0], both_w[:, both])
        pre[:, both] = value
        gate_value = value[:, :LANES]
        hidden[:, strip(n, LANES)] = (
            gate_value * jax.nn.sigmoid(gate_value) * value[:, LANES:]
        ).astype(BF16)

    receive(1)

    def send_back(i):
        each_peer(lambda q: give_back(i, q, me).start())
        back[i, mine] = part[i, mine]

    @loop(chunks)
    def _(c):
        @loop(CHUNK // STEP)
        def _(n):
            cols = strip(c * (CHUNK // STEP) + n, STEP)
            part[c, :, strip(n, STEP)] = dot(hidden[...], down_w[:, cols]).astype(BF16)

        send_back(c)

    passed(1)

    @loop(strips)
    def _(n):
        both = strip(n, 2 * LANES)
        hidden_grad = contract_last(rows[1], down_w[strip(n, LANES), :])
        value = pre[:, both]
        gate_value, up_value = value[:, :LANES], value[:, LANES:]
        sig = jax.nn.sigmoid(gate_value)
        pre_grad[:, strip(2 * n, LANES)] = (
            hidden_grad * up_value * sig * (1.0 + gate_value * (1.0 - sig))
        ).astype(BF16)
        pre_grad[:, strip(2 * n + 1, LANES)] = (hidden_grad * (gate_value * sig)).astype(BF16)

    stores = [
        pltpu.make_async_copy(src, dst, store_sem.at[i])
        for i, (src, dst) in enumerate(
            ((rows, rows_out), (hidden, hidden_out), (pre_grad, pre_grad_out))
        )
    ]
    for store in stores:
        store.start()

    def line_copy(i, source, where, target, send_line, peer):
        is_dot = isinstance(i, int)
        return pltpu.make_async_remote_copy(
            src_ref=source,
            dst_ref=dot_in.at[where] if is_dot else line_in.at[where, i],
            send_sem=send_line.at[i],
            recv_sem=line_sem.at[target, i],
            device_id={"etp": peer},
            device_id_type=MESH,
        )

    def own_of(i):
        return dot_own if isinstance(i, int) else line_own.at[i]

    def total_of(i):
        return dot_total if isinstance(i, int) else total_ref.at[i]

    def came(i, where):
        return dot_in.at[where] if isinstance(i, int) else line_in.at[where, i]

    def to_inner(i):
        return line_copy(i, own_of(i), kind, kind, inner_sem, inner)

    def to_outer(i):
        return line_copy(i, total_of(i), 1, 1, outer_sem, outer)

    def arrived(i, where):
        return line_copy(i, own_of(i), where, where, inner_sem, inner)

    def inward(i, value):
        own = own_of(i)

        @pl.when(has_outer)
        def _():
            arrived(i, 0).wait_recv()
            own[...] = (value + came(i, 0)[...].astype(F32)).astype(own.dtype)

        @pl.when(jnp.logical_not(has_outer))
        def _():
            own[...] = value.astype(own.dtype)

        to_inner(i).start()

    def outward(i):
        own, total = own_of(i), total_of(i)
        arrived(i, 1).wait_recv()

        @pl.when(center)
        def _():
            total[...] = (own[...].astype(F32) + came(i, 1)[...].astype(F32)).astype(own.dtype)

        @pl.when(jnp.logical_not(center))
        def _():
            total[...] = came(i, 1)[...]

        @pl.when(has_outer)
        def _():
            to_outer(i).start()

    @loop(chunks)
    def _(i):
        @loop(CHUNK // STEP)
        def _(n):
            rows_of = strip(i * (CHUNK // STEP) + n, STEP)
            part[chunks + i, :, strip(n, STEP)] = contract_last(
                pre_grad[...], both_w[rows_of, :]
            ).astype(BF16)

        send_back(chunks + i)

    @loop(chunks)
    def _(i):
        each_peer(lambda q: give_back(i, me, q).wait_recv())

        @loop(split)
        def _(n):
            at = i * split + n
            pairs = [dot(gather_mat[k], back[i, :, strip(n, LINE)]) for k in range(2)]
            value = grad_ref[:, strip(at, LINE)].astype(F32)
            for k in range(2):
                term = value * pairs[k]
                products[k] += sum(
                    term[:, s * LANES : (s + 1) * LANES] for s in range(LINE // LANES)
                )
            inward(at, weight_cols[0][:, :1] * pairs[0] + weight_cols[1][:, :1] * pairs[1])

            @pl.when(jnp.logical_and(center, at >= LAG))
            def _():
                outward(at - LAG)

    sums = [jnp.sum(products[k], axis=1, keepdims=True) for k in range(2)]
    lane = lax.broadcasted_iota(jnp.int32, (token_count, LANES), 1)
    inward(last, jnp.where(lane == 0, sums[0], jnp.where(lane == 1, sums[1], 0.0)).T[:8])

    @loop(items, chunks)
    def _(j):
        each_peer(lambda q: give_back(j, me, q).wait_recv())

        @loop(split)
        def _(n):
            at = j * split + n

            @pl.when(center)
            def _():
                outward(at - LAG)

            inward(at, dot(gather_mat[2], back[j, :, strip(n, LINE)]))

    loop(last, jnp.where(center, last - LAG, 0))(outward)
    outward(last)
    combine_ref[...] = dot_total[:2]

    for store in stores:
        store.wait()

    @each_peer
    def _(q):
        dispatch(0, q, me).wait_send()
        dispatch(1, q, me).wait_send()
        pass_on(0, q, parity).wait_send()
        pass_on(1, q, parity).wait_send()
        loop(items)(lambda i: give_back(i, q, me).wait_send())

    loop(last)(lambda i: to_inner(i).wait_send())
    to_inner(last).wait_send()

    @pl.when(has_outer)
    def _():
        loop(last)(lambda i: to_outer(i).wait_send())
        to_outer(last).wait_send()


def weight_grad_kernel(
    rows_ref,
    rows_grad_ref,
    hidden_ref,
    pre_grad_ref,
    mixed_ref,
    tokens_grad_ref,
    combine_ref,
    gate_out,
    up_out,
    down_out,
    mixed_out,
    tokens_grad_out,
    combine_out,
    hidden_t,
    rows_t,
):
    strips = hidden_ref.shape[1] // LANES

    def strip(n, width):
        return pl.ds(pl.multiple_of(n * width, width), width)

    def turn(n, carry):
        hidden_t[strip(n, LANES), :] = hidden_ref[:, strip(n, LANES)].T
        return carry

    @pl.when(pl.program_id(0) == 0)
    def _():
        lax.fori_loop(0, strips, turn, 0)

    mixed_out[...] = mixed_ref[0]
    tokens_grad_out[...] = tokens_grad_ref[0]
    combine_out[...] = combine_ref[...]
    rows_t[...] = rows_ref[0].T

    both = dot(rows_t[...], pre_grad_ref[...]).astype(BF16)
    for n in range(strips):
        one = slice(n * LANES, (n + 1) * LANES)
        gate_out[:, one] = both[:, 2 * n * LANES : (2 * n + 1) * LANES]
        up_out[:, one] = both[:, (2 * n + 1) * LANES : (2 * n + 2) * LANES]
    down_out[...] = dot(hidden_t[...], rows_grad_ref[0]).astype(BF16)


def weight_grads(rows, hidden, pre_grad, total, combine):
    _, places, features = rows.shape
    units = hidden.shape[1]
    chunks, token_count = total.shape[0] // 2, total.shape[1]
    split = LINE // STEP
    tall = pl.BlockSpec((STEP, units), lambda i: (i, 0))
    wide = pl.BlockSpec((units, STEP), lambda i: (0, i))
    token_cols = pl.BlockSpec((token_count, STEP), lambda i: (0, i))
    pair_sums = pl.BlockSpec((2, token_count), lambda i: (0, 0))
    return pl.pallas_call(
        weight_grad_kernel,
        grid=(features // STEP,),
        in_specs=[
            pl.BlockSpec((1, places, STEP), lambda i: (0, 0, i)),
            pl.BlockSpec((1, places, STEP), lambda i: (1, 0, i)),
            pl.BlockSpec((places, units), lambda i: (0, 0)),
            pl.BlockSpec((places, 2 * units), lambda i: (0, 0)),
            pl.BlockSpec((1, token_count, STEP), lambda i: (i // split, 0, i % split)),
            pl.BlockSpec((1, token_count, STEP), lambda i: (chunks + i // split, 0, i % split)),
            pair_sums,
        ],
        out_specs=[tall, tall, wide, token_cols, token_cols, pair_sums],
        out_shape=[
            jax.ShapeDtypeStruct((features, units), BF16),
            jax.ShapeDtypeStruct((features, units), BF16),
            jax.ShapeDtypeStruct((units, features), BF16),
            jax.ShapeDtypeStruct((token_count, features), BF16),
            jax.ShapeDtypeStruct((token_count, features), BF16),
            jax.ShapeDtypeStruct((2, token_count), F32),
        ],
        scratch_shapes=[pltpu.VMEM((units, places), BF16), pltpu.VMEM((STEP, places), BF16)],
        compiler_params=pltpu.CompilerParams(vmem_limit_bytes=60 << 20),
        cost_estimate=pl.CostEstimate(
            flops=6 * places * features * units,
            bytes_accessed=6 * features * units + 4 * places * features + 6 * places * units,
            transcendentals=0,
        ),
    )(rows, rows, hidden, pre_grad, total, total, combine)


def shards(experts, lines, tokens, out_grad, routes, combine_weights, w_gate, w_up, w_down):
    token_count, features = tokens.shape
    units = w_gate.shape[2]
    cap = token_count // 4
    places = experts * cap
    chunks = features // CHUNK
    items = 2 * chunks
    line_items = items * CHUNK // LINE
    vmem = pl.BlockSpec(memory_space=pltpu.VMEM)
    hbm = pl.BlockSpec(memory_space=pl.ANY)
    dma = pltpu.SemaphoreType.DMA
    total, combine, rows, hidden, pre_grad = pl.pallas_call(
        functools.partial(layer_kernel, experts, lines),
        in_specs=[vmem] * 4 + [hbm] * 3,
        out_specs=[vmem] * 2 + [hbm] * 3,
        out_shape=[
            jax.ShapeDtypeStruct((line_items, token_count, LINE), BF16),
            jax.ShapeDtypeStruct((2, token_count), F32),
            jax.ShapeDtypeStruct((2, places, features), BF16),
            jax.ShapeDtypeStruct((places, units), BF16),
            jax.ShapeDtypeStruct((places, 2 * units), BF16),
        ],
        scratch_shapes=[
            pltpu.VMEM((features, 2 * units), BF16),
            pltpu.VMEM((units, features), BF16),
            pltpu.VMEM((2, places, features), BF16),
            pltpu.VMEM((2, places, features), BF16),
            pltpu.VMEM((places, 2 * units), F32),
            pltpu.VMEM((places, units), BF16),
            pltpu.VMEM((places, 2 * units), BF16),
            pltpu.VMEM((3, places, token_count), BF16),
            pltpu.VMEM((3, token_count, places), BF16),
            pltpu.VMEM((2, token_count, LANES), F32),
            pltpu.VMEM((2, token_count, LANES), F32),
            pltpu.VMEM((items, places, CHUNK), BF16),
            pltpu.VMEM((items, places, CHUNK), BF16),
            pltpu.VMEM((line_items, token_count, LINE), BF16),
            pltpu.VMEM((2, line_items, token_count, LINE), BF16),
            pltpu.VMEM((8, token_count), F32),
            pltpu.VMEM((2, 8, token_count), F32),
            pltpu.VMEM((8, token_count), F32),
            dma((2 * (units // LANES) + 1,)),
            dma((3,)),
            dma((2, experts)),
            dma((2, experts)),
            dma((2, experts)),
            dma((2, experts)),
            dma((items, experts)),
            dma((items, experts)),
            dma((line_items + 1,)),
            dma((2, line_items + 1)),
            dma((line_items + 1,)),
        ],
        compiler_params=pltpu.CompilerParams(
            collective_id=0, has_side_effects=True, vmem_limit_bytes=56 << 20
        ),
        cost_estimate=pl.CostEstimate(
            flops=12 * places * features * units,
            bytes_accessed=6 * features * units,
            transcendentals=2 * places * units,
        ),
    )(tokens, out_grad, routes.T, combine_weights.T, w_gate[0], w_up[0], w_down[0])
    gate_wg, up_wg, down_wg, mixed, tokens_grad, combine = weight_grads(
        rows, hidden, pre_grad, total, combine
    )
    return mixed, tokens_grad, combine.T, gate_wg[None], up_wg[None], down_wg[None]


def solution(mesh):
    rows = P("expert", None)
    columns = P("expert", None, "etp")
    return jax.shard_map(
        functools.partial(shards, mesh.shape["expert"], mesh.shape["etp"]),
        mesh=mesh,
        in_specs=(rows, rows, rows, rows, columns, columns, P("expert", "etp", None)),
        out_specs=(rows, rows, rows, columns, columns, P("expert", "etp", None)),
        check_vma=False,
    )
```

```python
import functools

import jax
import jax.numpy as jnp
from jax import lax
from jax.experimental import pallas as pl
from jax.experimental.pallas import tpu as pltpu
from jax.sharding import PartitionSpec as P

MESH = pl.DeviceIdType.MESH
BF16 = jnp.bfloat16
F32 = jnp.float32
CHUNK = 512
LANES = 128
LAG = 3
LINE = 512
SHARED = 3 / 8
STEP = 256


def dot(left, right):
    return jnp.dot(left, right, preferred_element_type=F32)


def contract_last(left, right):
    return lax.dot_general(left, right, (((1,), (1,)), ((), ())), preferred_element_type=F32)


def contract_first(left, right):
    return lax.dot_general(left, right, (((0,), (0,)), ((), ())), preferred_element_type=F32)


def one_hot_places(routes_row, routes_col, cap, places):
    tokens = routes_row.shape[1]
    before_by = lax.broadcasted_iota(jnp.int32, (tokens, tokens), 0)
    before_at = lax.broadcasted_iota(jnp.int32, (tokens, tokens), 1)
    upper = (before_by < before_at).astype(F32).astype(BF16)
    lower = (before_by > before_at).astype(F32).astype(BF16)
    expert_down = lax.broadcasted_iota(jnp.int32, (LANES, tokens), 0)
    expert_across = lax.broadcasted_iota(jnp.int32, (tokens, LANES), 1)
    named_down = [(expert_down == routes_row[k : k + 1, :]).astype(F32) for k in range(2)]
    named_across = [
        (expert_across.astype(F32) == routes_col[:, k : k + 1]).astype(F32) for k in range(2)
    ]
    earlier_down = dot((named_down[0] + named_down[1]).astype(BF16), upper)
    earlier_across = dot(lower, (named_across[0] + named_across[1]).astype(BF16))
    start_down = earlier_down + expert_down.astype(F32) * cap
    start_across = earlier_across + expert_across.astype(F32) * cap
    place_down = lax.broadcasted_iota(jnp.int32, (places, tokens), 0).astype(F32)
    place_across = lax.broadcasted_iota(jnp.int32, (tokens, places), 1).astype(F32)
    scatter, gather = [], []
    for k in range(2):
        row = jnp.sum(named_down[k] * start_down, axis=0, keepdims=True)
        col = jnp.sum(named_across[k] * start_across, axis=1, keepdims=True)
        scatter.append((place_down == row).astype(F32).astype(BF16))
        gather.append((place_across == col).astype(F32).astype(BF16))
    return scatter, gather


def layer_kernel(
    experts,
    lines,
    tokens_ref,
    grad_ref,
    routes_ref,
    weights_ref,
    gate_hbm,
    up_hbm,
    down_hbm,
    total_ref,
    combine_ref,
    rows_out,
    hidden_out,
    pre_grad_out,
    both_w,
    down_w,
    send,
    rows,
    pre,
    hidden,
    pre_grad,
    scatter_mat,
    gather_mat,
    weight_cols,
    products,
    part,
    back,
    line_own,
    line_in,
    dot_own,
    dot_in,
    dot_total,
    load_sem,
    store_sem,
    send_sem,
    recv_sem,
    pass_send_sem,
    pass_recv_sem,
    part_sem,
    back_sem,
    inner_sem,
    line_sem,
    outer_sem,
):
    token_count, features = tokens_ref.shape
    cap = token_count // 4
    places = experts * cap
    chunks = features // CHUNK
    items = 2 * chunks
    split = CHUNK // LINE
    last = items * split
    shared = int(features * SHARED) // LANES * LANES
    kept = features - shared
    strips = hidden.shape[1] // LANES
    me = lax.axis_index("expert")
    z = lax.axis_index("etp")
    half = lines // 2
    side = 1 - z // half
    inner = z + 2 * side - 1
    outer = z - 2 * side + 1
    has_outer = jnp.logical_and(z > 0, z < lines - 1)
    center = jnp.logical_or(z == half - 1, z == half)
    kind = jnp.where(center, 1, 0)
    parity = lax.rem(z, 2)
    partner = z + 1 - 2 * parity

    def strip(n, width):
        return pl.ds(pl.multiple_of(n * width, width), width)

    def load(i, n):
        source = (gate_hbm, up_hbm)[i]
        return pltpu.make_async_copy(
            source.at[:, strip(n, LANES)],
            both_w.at[:, strip(2 * n + i, LANES)],
            load_sem.at[2 * n + i],
        )

    def loop(count, start=0):
        return lambda body: lax.fori_loop(start, count, lambda i, c: (body(i), c)[1], 0)

    load_down = pltpu.make_async_copy(down_hbm, down_w, load_sem.at[2 * strips])

    @loop(strips)
    def _(n):
        load(0, n).start()
        load(1, n).start()

    load_down.start()

    barrier = pltpu.get_barrier_semaphore()

    def each_peer(action):
        loop(experts, 1)(lambda d: action(lax.rem(me + d, experts)))

    @each_peer
    def _(peer):
        pl.semaphore_signal(barrier, inc=1, device_id={"expert": peer}, device_id_type=MESH)

    pl.semaphore_signal(barrier, inc=1, device_id={"etp": inner}, device_id_type=MESH)

    @pl.when(has_outer)
    def _():
        pl.semaphore_signal(barrier, inc=1, device_id={"etp": outer}, device_id_type=MESH)

    def block_of(index):
        return strip(index, cap)

    mine = block_of(me)

    def dispatch(i, peer, owner):
        cols = pl.ds(pl.multiple_of(parity * shared, LANES), kept)
        return pltpu.make_async_remote_copy(
            src_ref=send.at[i, block_of(peer), cols],
            dst_ref=rows.at[i, block_of(owner), cols],
            send_sem=send_sem.at[i, peer],
            recv_sem=recv_sem.at[i, owner],
            device_id={"expert": peer},
            device_id_type=MESH,
        )

    def pass_on(i, owner, side_of):
        cols = pl.ds(pl.multiple_of(side_of * kept, LANES), shared)
        return pltpu.make_async_remote_copy(
            src_ref=rows.at[i, block_of(owner), cols],
            dst_ref=rows.at[i, block_of(owner), cols],
            send_sem=pass_send_sem.at[i, owner],
            recv_sem=pass_recv_sem.at[i, owner],
            device_id={"etp": partner},
            device_id_type=MESH,
        )

    def receive(i):
        def one(d):
            q = lax.rem(me + experts - d, experts)
            dispatch(i, me, q).wait_recv()
            pass_on(i, q, parity).start()

        loop(experts, 1)(one)

    def passed(i):
        each_peer(lambda q: pass_on(i, q, 1 - parity).wait_recv())

    def give_back(i, peer, owner):
        return pltpu.make_async_remote_copy(
            src_ref=part.at[i, block_of(peer)],
            dst_ref=back.at[i, block_of(owner)],
            send_sem=part_sem.at[i, peer],
            recv_sem=back_sem.at[i, owner],
            device_id={"expert": peer},
            device_id_type=MESH,
        )

    sub = lax.broadcasted_iota(jnp.int32, (LANES, token_count), 0)
    table = jnp.where(sub == 0, routes_ref[0:1, :], routes_ref[1:2, :]).astype(F32)
    table = jnp.where(sub == 2, weights_ref[0:1, :], table)
    table = jnp.where(sub == 3, weights_ref[1:2, :], table).T
    scatter, gather = one_hot_places(routes_ref[...], table, cap, places)
    for k in range(2):
        scatter_mat[k] = scatter[k]
        gather_mat[k] = gather[k]
        weight_cols[k] = jnp.broadcast_to(table[:, 2 + k : 3 + k], (token_count, LANES))
    products[...] = jnp.zeros_like(products)
    scatter_mat[2] = scatter[0] + scatter[1]
    gather_mat[2] = gather[0] + gather[1]

    @loop(features // STEP)
    def _(c):
        cols = strip(c, STEP)
        send[0, :, cols] = dot(scatter_mat[2], tokens_ref[:, cols]).astype(BF16)

    pl.semaphore_wait(barrier, experts + jnp.where(has_outer, 1, 0))
    each_peer(lambda q: dispatch(0, q, me).start())
    rows[0, mine] = send[0, mine]

    @loop(features // STEP)
    def _(c):
        cols = strip(c, STEP)
        value = grad_ref[:, cols].astype(F32)
        scaled = [(weight_cols[k][:, :1] * value).astype(BF16) for k in range(2)]
        send[1, :, cols] = (dot(scatter_mat[0], scaled[0]) + dot(scatter_mat[1], scaled[1])).astype(
            BF16
        )

    each_peer(lambda q: dispatch(1, q, me).start())
    rows[1, mine] = send[1, mine]

    @loop(strips)
    def _(n):
        load(0, n).wait()
        load(1, n).wait()

    load_down.wait()
    receive(0)
    passed(0)

    @loop(strips)
    def _(n):
        both = strip(n, 2 * LANES)
        value = dot(rows[0], both_w[:, both])
        pre[:, both] = value
        gate_value = value[:, :LANES]
        hidden[:, strip(n, LANES)] = (
            gate_value * jax.nn.sigmoid(gate_value) * value[:, LANES:]
        ).astype(BF16)

    def send_back(i):
        each_peer(lambda q: give_back(i, q, me).start())
        back[i, mine] = part[i, mine]

    @loop(chunks)
    def _(c):
        @loop(CHUNK // STEP)
        def _(n):
            cols = strip(c * (CHUNK // STEP) + n, STEP)
            part[c, :, strip(n, STEP)] = dot(hidden[...], down_w[:, cols]).astype(BF16)

        send_back(c)

    receive(1)
    passed(1)

    @loop(strips)
    def _(n):
        both = strip(n, 2 * LANES)
        hidden_grad = contract_last(rows[1], down_w[strip(n, LANES), :])
        value = pre[:, both]
        gate_value, up_value = value[:, :LANES], value[:, LANES:]
        sig = jax.nn.sigmoid(gate_value)
        pre_grad[:, strip(2 * n, LANES)] = (
            hidden_grad * up_value * sig * (1.0 + gate_value * (1.0 - sig))
        ).astype(BF16)
        pre_grad[:, strip(2 * n + 1, LANES)] = (hidden_grad * (gate_value * sig)).astype(BF16)

    stores = [
        pltpu.make_async_copy(src, dst, store_sem.at[i])
        for i, (src, dst) in enumerate(
            ((rows, rows_out), (hidden, hidden_out), (pre_grad, pre_grad_out))
        )
    ]
    for store in stores:
        store.start()

    def line_copy(i, source, where, target, send_line, peer):
        is_dot = isinstance(i, int)
        return pltpu.make_async_remote_copy(
            src_ref=source,
            dst_ref=dot_in.at[where] if is_dot else line_in.at[where, i],
            send_sem=send_line.at[i],
            recv_sem=line_sem.at[target, i],
            device_id={"etp": peer},
            device_id_type=MESH,
        )

    def own_of(i):
        return dot_own if isinstance(i, int) else line_own.at[i]

    def total_of(i):
        return dot_total if isinstance(i, int) else total_ref.at[i]

    def came(i, where):
        return dot_in.at[where] if isinstance(i, int) else line_in.at[where, i]

    def to_inner(i):
        return line_copy(i, own_of(i), kind, kind, inner_sem, inner)

    def to_outer(i):
        return line_copy(i, total_of(i), 1, 1, outer_sem, outer)

    def arrived(i, where):
        return line_copy(i, own_of(i), where, where, inner_sem, inner)

    def inward(i, value):
        own = own_of(i)

        @pl.when(has_outer)
        def _():
            arrived(i, 0).wait_recv()
            own[...] = (value + came(i, 0)[...].astype(F32)).astype(own.dtype)

        @pl.when(jnp.logical_not(has_outer))
        def _():
            own[...] = value.astype(own.dtype)

        to_inner(i).start()

    def outward(i):
        own, total = own_of(i), total_of(i)
        arrived(i, 1).wait_recv()

        @pl.when(center)
        def _():
            total[...] = (own[...].astype(F32) + came(i, 1)[...].astype(F32)).astype(own.dtype)

        @pl.when(jnp.logical_not(center))
        def _():
            total[...] = came(i, 1)[...]

        @pl.when(has_outer)
        def _():
            to_outer(i).start()

    @loop(chunks)
    def _(i):
        @loop(CHUNK // STEP)
        def _(n):
            rows_of = strip(i * (CHUNK // STEP) + n, STEP)
            part[chunks + i, :, strip(n, STEP)] = contract_last(
                pre_grad[...], both_w[rows_of, :]
            ).astype(BF16)

        send_back(chunks + i)

    @loop(chunks)
    def _(i):
        each_peer(lambda q: give_back(i, me, q).wait_recv())

        @loop(split)
        def _(n):
            at = i * split + n
            pairs = [dot(gather_mat[k], back[i, :, strip(n, LINE)]) for k in range(2)]
            value = grad_ref[:, strip(at, LINE)].astype(F32)
            for k in range(2):
                term = value * pairs[k]
                products[k] += sum(
                    term[:, s * LANES : (s + 1) * LANES] for s in range(LINE // LANES)
                )
            inward(at, weight_cols[0][:, :1] * pairs[0] + weight_cols[1][:, :1] * pairs[1])

            @pl.when(jnp.logical_and(center, at >= LAG))
            def _():
                outward(at - LAG)

    sums = [jnp.sum(products[k], axis=1, keepdims=True) for k in range(2)]
    lane = lax.broadcasted_iota(jnp.int32, (token_count, LANES), 1)
    inward(last, jnp.where(lane == 0, sums[0], jnp.where(lane == 1, sums[1], 0.0)).T[:8])

    @loop(items, chunks)
    def _(j):
        each_peer(lambda q: give_back(j, me, q).wait_recv())

        @loop(split)
        def _(n):
            at = j * split + n

            @pl.when(center)
            def _():
                outward(at - LAG)

            inward(at, dot(gather_mat[2], back[j, :, strip(n, LINE)]))

    loop(last, jnp.where(center, last - LAG, 0))(outward)
    outward(last)
    combine_ref[...] = dot_total[:2]

    for store in stores:
        store.wait()

    @each_peer
    def _(q):
        dispatch(0, q, me).wait_send()
        dispatch(1, q, me).wait_send()
        pass_on(0, q, parity).wait_send()
        pass_on(1, q, parity).wait_send()
        loop(items)(lambda i: give_back(i, q, me).wait_send())

    loop(last)(lambda i: to_inner(i).wait_send())
    to_inner(last).wait_send()

    @pl.when(has_outer)
    def _():
        loop(last)(lambda i: to_outer(i).wait_send())
        to_outer(last).wait_send()


def weight_grad_kernel(
    rows_ref,
    rows_grad_ref,
    hidden_ref,
    pre_grad_ref,
    mixed_ref,
    tokens_grad_ref,
    combine_ref,
    gate_out,
    up_out,
    down_out,
    mixed_out,
    tokens_grad_out,
    combine_out,
    hidden_t,
    rows_t,
):
    strips = hidden_ref.shape[1] // LANES

    def strip(n, width):
        return pl.ds(pl.multiple_of(n * width, width), width)

    def turn(n, carry):
        hidden_t[strip(n, LANES), :] = hidden_ref[:, strip(n, LANES)].T
        return carry

    @pl.when(pl.program_id(0) == 0)
    def _():
        lax.fori_loop(0, strips, turn, 0)

    mixed_out[...] = mixed_ref[0]
    tokens_grad_out[...] = tokens_grad_ref[0]
    combine_out[...] = combine_ref[...]
    rows_t[...] = rows_ref[0].T

    both = dot(rows_t[...], pre_grad_ref[...]).astype(BF16)
    for n in range(strips):
        one = slice(n * LANES, (n + 1) * LANES)
        gate_out[:, one] = both[:, 2 * n * LANES : (2 * n + 1) * LANES]
        up_out[:, one] = both[:, (2 * n + 1) * LANES : (2 * n + 2) * LANES]
    down_out[...] = dot(hidden_t[...], rows_grad_ref[0]).astype(BF16)


def weight_grads(rows, hidden, pre_grad, total, combine):
    _, places, features = rows.shape
    units = hidden.shape[1]
    chunks, token_count = total.shape[0] // 2, total.shape[1]
    split = LINE // STEP
    tall = pl.BlockSpec((STEP, units), lambda i: (i, 0))
    wide = pl.BlockSpec((units, STEP), lambda i: (0, i))
    token_cols = pl.BlockSpec((token_count, STEP), lambda i: (0, i))
    pair_sums = pl.BlockSpec((2, token_count), lambda i: (0, 0))
    return pl.pallas_call(
        weight_grad_kernel,
        grid=(features // STEP,),
        in_specs=[
            pl.BlockSpec((1, places, STEP), lambda i: (0, 0, i)),
            pl.BlockSpec((1, places, STEP), lambda i: (1, 0, i)),
            pl.BlockSpec((places, units), lambda i: (0, 0)),
            pl.BlockSpec((places, 2 * units), lambda i: (0, 0)),
            pl.BlockSpec((1, token_count, STEP), lambda i: (i // split, 0, i % split)),
            pl.BlockSpec((1, token_count, STEP), lambda i: (chunks + i // split, 0, i % split)),
            pair_sums,
        ],
        out_specs=[tall, tall, wide, token_cols, token_cols, pair_sums],
        out_shape=[
            jax.ShapeDtypeStruct((features, units), BF16),
            jax.ShapeDtypeStruct((features, units), BF16),
            jax.ShapeDtypeStruct((units, features), BF16),
            jax.ShapeDtypeStruct((token_count, features), BF16),
            jax.ShapeDtypeStruct((token_count, features), BF16),
            jax.ShapeDtypeStruct((2, token_count), F32),
        ],
        scratch_shapes=[pltpu.VMEM((units, places), BF16), pltpu.VMEM((STEP, places), BF16)],
        compiler_params=pltpu.CompilerParams(vmem_limit_bytes=60 << 20),
        cost_estimate=pl.CostEstimate(
            flops=6 * places * features * units,
            bytes_accessed=6 * features * units + 4 * places * features + 6 * places * units,
            transcendentals=0,
        ),
    )(rows, rows, hidden, pre_grad, total, total, combine)


def shards(experts, lines, tokens, out_grad, routes, combine_weights, w_gate, w_up, w_down):
    token_count, features = tokens.shape
    units = w_gate.shape[2]
    cap = token_count // 4
    places = experts * cap
    chunks = features // CHUNK
    items = 2 * chunks
    line_items = items * CHUNK // LINE
    vmem = pl.BlockSpec(memory_space=pltpu.VMEM)
    hbm = pl.BlockSpec(memory_space=pl.ANY)
    dma = pltpu.SemaphoreType.DMA
    total, combine, rows, hidden, pre_grad = pl.pallas_call(
        functools.partial(layer_kernel, experts, lines),
        in_specs=[vmem] * 4 + [hbm] * 3,
        out_specs=[vmem] * 2 + [hbm] * 3,
        out_shape=[
            jax.ShapeDtypeStruct((line_items, token_count, LINE), BF16),
            jax.ShapeDtypeStruct((2, token_count), F32),
            jax.ShapeDtypeStruct((2, places, features), BF16),
            jax.ShapeDtypeStruct((places, units), BF16),
            jax.ShapeDtypeStruct((places, 2 * units), BF16),
        ],
        scratch_shapes=[
            pltpu.VMEM((features, 2 * units), BF16),
            pltpu.VMEM((units, features), BF16),
            pltpu.VMEM((2, places, features), BF16),
            pltpu.VMEM((2, places, features), BF16),
            pltpu.VMEM((places, 2 * units), F32),
            pltpu.VMEM((places, units), BF16),
            pltpu.VMEM((places, 2 * units), BF16),
            pltpu.VMEM((3, places, token_count), BF16),
            pltpu.VMEM((3, token_count, places), BF16),
            pltpu.VMEM((2, token_count, LANES), F32),
            pltpu.VMEM((2, token_count, LANES), F32),
            pltpu.VMEM((items, places, CHUNK), BF16),
            pltpu.VMEM((items, places, CHUNK), BF16),
            pltpu.VMEM((line_items, token_count, LINE), BF16),
            pltpu.VMEM((2, line_items, token_count, LINE), BF16),
            pltpu.VMEM((8, token_count), F32),
            pltpu.VMEM((2, 8, token_count), F32),
            pltpu.VMEM((8, token_count), F32),
            dma((2 * (units // LANES) + 1,)),
            dma((3,)),
            dma((2, experts)),
            dma((2, experts)),
            dma((2, experts)),
            dma((2, experts)),
            dma((items, experts)),
            dma((items, experts)),
            dma((line_items + 1,)),
            dma((2, line_items + 1)),
            dma((line_items + 1,)),
        ],
        compiler_params=pltpu.CompilerParams(
            collective_id=0, has_side_effects=True, vmem_limit_bytes=56 << 20
        ),
        cost_estimate=pl.CostEstimate(
            flops=12 * places * features * units,
            bytes_accessed=6 * features * units,
            transcendentals=2 * places * units,
        ),
    )(tokens, out_grad, routes.T, combine_weights.T, w_gate[0], w_up[0], w_down[0])
    gate_wg, up_wg, down_wg, mixed, tokens_grad, combine = weight_grads(
        rows, hidden, pre_grad, total, combine
    )
    return mixed, tokens_grad, combine.T, gate_wg[None], up_wg[None], down_wg[None]


def solution(mesh):
    rows = P("expert", None)
    columns = P("expert", None, "etp")
    return jax.shard_map(
        functools.partial(shards, mesh.shape["expert"], mesh.shape["etp"]),
        mesh=mesh,
        in_specs=(rows, rows, rows, rows, columns, columns, P("expert", "etp", None)),
        out_specs=(rows, rows, rows, columns, columns, P("expert", "etp", None)),
        check_vma=False,
    )
```
